32 devices in a mesh: grp: 8 (over y, x, core), fsdp: 4 (over z).
Axes of the slice: x: 2, y: 2, z: 4, core: 2. Of those that a mesh axis runs over, the one named last changes fastest.
Arguments:
- inputs: bfloat16 [8192, 8192], P(('grp', 'fsdp')), may hold values from -6 to 6
- upstream: bfloat16 [8192, 1024], P(('grp', 'fsdp')), may hold values from -12 to 12
- value_weight: bfloat16 [8192, 1024], P('fsdp'), may hold values from -0.0625 to 0.0625
- adapter_in: bfloat16 [8192, 8], replicated, may hold values from -0.0625 to 0.0625
- adapter_out: bfloat16 [8, 1024], replicated, may hold values from -0.1875 to 0.1875
- sign_seed: int32 [1], replicated, may hold values from 0 to 1073741823
Outputs:
- input_grads: bfloat16 [8192, 8192], P(('grp', 'fsdp'))
- features: float32 [32, 4096], P(('grp', 'fsdp'))
- mean_grad: float32 [73728], P('fsdp')
The draws below stay inside these ranges and needn't reach their ends.
All inputs are finite; a program needn't handle non-finite values.
Results may differ from the reference program's by a relative error of at most 0.005.
Values may be sent and summed in bfloat16 or wider, within the bound.
No kernel may reach another device: no remote copies, remote signals or barrier semaphores. Data moves between devices by JAX's collectives and lax.ppermute only.
A program may use at most 128 MiB of HBM per device.

```python
import math
import jax
import jax.numpy as jnp
from jax import lax

D = 8192
KV = 1024
R = 8
PROJ = 4096
TOK_DEV = 256
PAIRS = 32
TOKENS = 8192
NPARAM = 73728


def shard_levels(own_key, shape, shards, low, top_value):
    factor_of = 1.0
    for axis_at, blocks in shards:
        heights = jax.random.uniform(jax.random.fold_in(jax.random.fold_in(own_key, 6), axis_at), (blocks,), jnp.float32, low / len(shards), top_value / len(shards))
        factor_of = factor_of * jnp.repeat(jnp.exp(heights), shape[axis_at] // blocks).reshape((-1,) + (1,) * (len(shape) - 1 - axis_at))
    return factor_of


def gaussian(key, shape, scale, reach, shards=(), kind=jnp.bfloat16):
    result = scale * jax.random.normal(key, shape, jnp.float32)
    if shards:
        result = result * shard_levels(key, shape, shards, -0.22, 0.18)
    return jnp.clip(result, -reach, reach).astype(kind)


def setup_inputs(seed: int = 0) -> dict:
    key_list = jax.random.split(jax.random.key(seed), 7)
    return {
        "inputs": gaussian(key_list[0], (TOKENS, D), 1.0, 6.0, ((0, 32),)),
        "upstream": gaussian(key_list[1], (TOKENS, KV), 2.0, 12.0, ((0, 32),)),
        "value_weight": gaussian(key_list[2], (D, KV), D ** -0.5, 0.0625, ((0, 4),)),
        "adapter_in": gaussian(key_list[3], (D, R), D ** -0.5, 0.0625),
        "adapter_out": gaussian(key_list[4], (R, KV), KV ** -0.5, 0.1875),
        "sign_seed": jax.random.randint(key_list[5], (1,), 0, 1073741824).astype(jnp.int32),
    }


lowrank_scale_factor = 2.0

def contract_last(left, right):
    return lax.dot_general(left, right, (((1,), (1,)), ((), ())), preferred_element_type=jnp.float32)

def leading_contraction(left, right):
    return lax.dot_general(left, right, (((0,), (0,)), ((), ())), preferred_element_type=jnp.float32)

def make_signs(start, count, width, seed_value):
    rows = start + lax.broadcasted_iota(jnp.int32, (count, 1), 0)
    columns = lax.broadcasted_iota(jnp.int32, (1, width), 1)
    mixed = rows * -1640531535 + columns * -2048144789 + seed_value * 668265263
    mixed = mixed ^ mixed >> 15 & 131071
    mixed = mixed * -1028477387
    mixed = mixed ^ mixed >> 13 & 524287
    return (1 - 2 * (mixed >> 16 & 1)).astype(jnp.bfloat16)

def reference(inputs, upstream, value_weight, adapter_in, adapter_out, sign_seed):
    adapter_expanded = adapter_in.astype(jnp.float32)
    pair_inputs = inputs.reshape(PAIRS, TOK_DEV, D)
    pair_upstream = upstream.reshape(PAIRS, TOK_DEV, KV)

    def one_pair(operands):
        rows_in, lifted_rows = operands
        passed_along = contract_last(lifted_rows, adapter_out)
        main_part = contract_last(lifted_rows, value_weight)
        lowrank_portion = jnp.dot(lowrank_scale_factor * passed_along, adapter_expanded.T, precision=lax.Precision.HIGHEST)
        grads_rows = (main_part + lowrank_portion).astype(jnp.bfloat16)
        rescaled_values = (lowrank_scale_factor * passed_along).astype(jnp.bfloat16)
        rank_reduced = jnp.dot(rows_in, adapter_in, preferred_element_type=jnp.float32).astype(jnp.bfloat16)
        grad_in = leading_contraction(rows_in, rescaled_values)
        output_gradient = lowrank_scale_factor * leading_contraction(rank_reduced, lifted_rows)
        flat = jnp.concatenate([grad_in.reshape(-1), output_gradient.reshape(-1)]).astype(jnp.bfloat16)
        return (grads_rows, flat)
    grads_all, pair_grad = lax.map(one_pair, (pair_inputs, pair_upstream))
    input_grads = grads_all.reshape(TOKENS, D)
    block = math.gcd(NPARAM, 4096)
    seed_value = sign_seed[0]

    def add_block(total, block_index):
        offset = block_index * block
        part = lax.dynamic_slice_in_dim(pair_grad, offset, block, 1)
        signs = make_signs(offset, block, PROJ, seed_value)
        return (total + jnp.dot(part, signs, preferred_element_type=jnp.float32), None)
    raw, unused = lax.scan(add_block, jnp.zeros((PAIRS, PROJ), jnp.float32), jnp.arange(NPARAM // block, dtype=jnp.int32))
    features = raw * lax.rsqrt(lax.optimization_barrier(jnp.mean(raw * raw, axis=1, keepdims=True)) + 1e-06)
    mean_grad = lax.optimization_barrier(jnp.sum(pair_grad.astype(jnp.float32), axis=0)) / PAIRS
    return (input_grads, features, mean_grad)
```

```python
import math

import jax
import jax.numpy as jnp
from jax import lax
from jax.sharding import PartitionSpec as P

PROJ = 4096

lowrank_scale_factor = 2.0


def contract_last(left, right):
    return lax.dot_general(
        left, right, (((1,), (1,)), ((), ())), preferred_element_type=jnp.float32
    )


def leading_contraction(left, right):
    return lax.dot_general(
        left, right, (((0,), (0,)), ((), ())), preferred_element_type=jnp.float32
    )


def make_signs(start, count, width, seed_value):
    rows = start + lax.broadcasted_iota(jnp.int32, (count, 1), 0)
    columns = lax.broadcasted_iota(jnp.int32, (1, width), 1)
    mixed = rows * -1640531535 + columns * -2048144789 + seed_value * 668265263
    mixed = mixed ^ lax.shift_right_logical(mixed, 15)
    mixed = mixed * 181057748
    mixed = mixed ^ lax.shift_left(mixed, 13)
    return jnp.where(mixed < 0, -1.0, 1.0).astype(jnp.bfloat16)


def per_device(inputs, upstream, value_weight, adapter_in, adapter_out, sign_seed):
    both = ("fsdp", "grp")
    groups = lax.axis_size("fsdp")
    members = lax.axis_size("grp")
    passed_along = contract_last(upstream, adapter_out)
    adapter_expanded = adapter_in.astype(jnp.float32)
    col_count = value_weight.shape[0]
    adapter_slice = lax.dynamic_slice_in_dim(
        adapter_expanded, lax.axis_index("fsdp") * col_count, col_count, 0
    )
    piece = lax.all_gather(upstream, "fsdp", axis=0, tiled=True)
    main_part = contract_last(piece, value_weight)
    piece_through = contract_last(piece, adapter_out)
    lowrank_portion = jnp.dot(
        lowrank_scale_factor * piece_through, adapter_slice.T, precision=lax.Precision.HIGHEST
    )
    columns = (main_part + lowrank_portion).astype(jnp.bfloat16)
    input_grads = lax.all_to_all(columns, "fsdp", split_axis=0, concat_axis=1, tiled=True)

    rescaled_values = (lowrank_scale_factor * passed_along).astype(jnp.bfloat16)
    rank_reduced = jnp.dot(inputs, adapter_in, preferred_element_type=jnp.float32).astype(
        jnp.bfloat16
    )
    grad_in = leading_contraction(inputs, rescaled_values)
    output_gradient = lowrank_scale_factor * leading_contraction(rank_reduced, upstream)
    flat = jnp.concatenate([grad_in.reshape(-1), output_gradient.reshape(-1)]).astype(jnp.bfloat16)
    devices = groups * members
    slice_len = flat.shape[0] // devices
    received = lax.all_to_all(
        flat.reshape(devices, slice_len), both, split_axis=0, concat_axis=0, tiled=True
    )
    local_total = jnp.sum(received.astype(jnp.float32), axis=0) / devices
    mean_grad = lax.all_to_all(
        jnp.broadcast_to(local_total, (members, slice_len)), "grp", split_axis=0, concat_axis=0, tiled=True
    ).reshape(-1)

    first_row = (lax.axis_index("fsdp") * members + lax.axis_index("grp")) * slice_len
    signs = make_signs(first_row, slice_len, PROJ, sign_seed[0])
    partial_feats = jnp.dot(received, signs, preferred_element_type=jnp.float32)
    parts = lax.all_to_all(partial_feats, both, split_axis=0, concat_axis=0, tiled=True)
    raw = jnp.sum(parts, axis=0, keepdims=True)
    features = raw * lax.rsqrt(jnp.mean(raw * raw, axis=1, keepdims=True) + 1e-06)
    return (input_grads, features, mean_grad)


def solution(mesh):
    return jax.shard_map(
        per_device,
        mesh=mesh,
        in_specs=(
            P(("grp", "fsdp"), None),
            P(("grp", "fsdp"), None),
            P("fsdp", None),
            P(),
            P(),
            P(),
        ),
        out_specs=(P(("grp", "fsdp"), None), P(("grp", "fsdp"), None), P("fsdp")),
        check_vma=False,
    )
```

```python
import functools

import jax
import jax.numpy as jnp
from jax import lax
from jax.experimental import pallas as pl
from jax.experimental.pallas import tpu as pltpu
from jax.sharding import PartitionSpec as P

PROJ = 4096

lowrank_scale_factor = 2.0


def contract_last(left, right):
    return lax.dot_general(
        left, right, (((1,), (1,)), ((), ())), preferred_element_type=jnp.float32
    )


def leading_contraction(left, right):
    return lax.dot_general(
        left, right, (((0,), (0,)), ((), ())), preferred_element_type=jnp.float32
    )


def make_signs(start, count, width, seed_value):
    rows = start + lax.broadcasted_iota(jnp.int32, (count, 1), 0)
    columns = lax.broadcasted_iota(jnp.int32, (1, width), 1)
    mixed = rows * -1640531535 + columns * -2048144789 + seed_value * 668265263
    mixed = mixed ^ lax.shift_right_logical(mixed, 15)
    mixed = mixed * 181057748
    mixed = mixed ^ lax.shift_left(mixed, 13)
    return jnp.where(mixed < 0, -1.0, 1.0).astype(jnp.bfloat16)


def split_pair(tokens, adapter_out):
    through = lowrank_scale_factor * contract_last(tokens, adapter_out)
    high = through.astype(jnp.bfloat16)
    low = (through - high.astype(jnp.float32)).astype(jnp.bfloat16)
    return jnp.concatenate([high, low], axis=1)


def own_kernel(up_ref, weight_ref, double_ref, out_adapter_ref, out_ref, pair_ref):
    @pl.when(pl.program_id(0) == 0)
    def _():
        pair_ref[...] = split_pair(up_ref[...], out_adapter_ref[...])

    total = contract_last(up_ref[...], weight_ref[...])
    total += contract_last(pair_ref[...], double_ref[...])
    out_ref[...] = total.astype(out_ref.dtype)


def own_columns(upstream, weight, double, adapter_out):
    tokens, depth = upstream.shape
    columns = weight.shape[0]
    block = min(512, columns)
    rank2 = double.shape[1]
    return pl.pallas_call(
        own_kernel,
        grid=(columns // block,),
        in_specs=[
            pl.BlockSpec((tokens, depth), lambda i: (0, 0)),
            pl.BlockSpec((block, depth), lambda i: (i, 0)),
            pl.BlockSpec((block, rank2), lambda i: (i, 0)),
            pl.BlockSpec(adapter_out.shape, lambda i: (0, 0)),
        ],
        out_specs=pl.BlockSpec((tokens, block), lambda i: (0, i)),
        out_shape=jax.ShapeDtypeStruct((tokens, columns), jnp.bfloat16),
        scratch_shapes=[pltpu.VMEM((tokens, rank2), jnp.bfloat16)],
        cost_estimate=pl.CostEstimate(
            flops=2 * tokens * depth * columns,
            bytes_accessed=2 * (tokens * depth + columns * depth + tokens * columns),
            transcendentals=0,
        ),
    )(upstream, weight, double, adapter_out)


def pair_kernel(even_ref, odd_ref, out_adapter_ref, even_pair_ref, odd_pair_ref):
    even_pair_ref[0] = split_pair(even_ref[0], out_adapter_ref[...])
    odd_pair_ref[0] = split_pair(odd_ref[0], out_adapter_ref[...])


def plane_pairs(even, odd, adapter_out):
    chips, tokens, depth = even.shape
    rank2 = 2 * adapter_out.shape[0]
    block = pl.BlockSpec((1, tokens, depth), lambda i: (i, 0, 0))
    pairs = pl.BlockSpec((1, tokens, rank2), lambda i: (i, 0, 0))
    shape = jax.ShapeDtypeStruct((chips, tokens, rank2), jnp.bfloat16)
    return pl.pallas_call(
        pair_kernel,
        grid=(chips,),
        in_specs=[block, block, pl.BlockSpec(adapter_out.shape, lambda i: (0, 0))],
        out_specs=[pairs, pairs],
        out_shape=[shape, shape],
        cost_estimate=pl.CostEstimate(
            flops=4 * chips * tokens * depth * 128, bytes_accessed=4 * chips * tokens * depth, transcendentals=0
        ),
    )(even, odd, adapter_out)


def piece_kernel(member_ref, even_ref, odd_ref, even_pair_ref, odd_pair_ref, weight_ref, double_ref, out_ref):
    core = lax.rem(member_ref[0], 2)
    for place, tokens, pair in ((core, even_ref, even_pair_ref), (1 - core, odd_ref, odd_pair_ref)):
        total = contract_last(tokens[0], weight_ref[...])
        total += contract_last(pair[0], double_ref[...])
        out_ref[0, place] = total.astype(out_ref.dtype)


def piece_columns(member, even, odd, even_pair, odd_pair, weight, double):
    chips, tokens, depth = even.shape
    width = weight.shape[0]
    rank2 = double.shape[1]
    block = pl.BlockSpec((1, tokens, depth), lambda i, m: (i, 0, 0))
    pairs = pl.BlockSpec((1, tokens, rank2), lambda i, m: (i, 0, 0))
    return pl.pallas_call(
        piece_kernel,
        grid_spec=pltpu.PrefetchScalarGridSpec(
            num_scalar_prefetch=1,
            grid=(chips,),
            in_specs=[
                block,
                block,
                pairs,
                pairs,
                pl.BlockSpec((width, depth), lambda i, m: (0, 0)),
                pl.BlockSpec((width, rank2), lambda i, m: (0, 0)),
            ],
            out_specs=pl.BlockSpec(
                (1, 2, tokens, width), lambda i, m: (lax.bitwise_xor(i, lax.div(m[0], 2)), 0, 0, 0)
            ),
        ),
        out_shape=jax.ShapeDtypeStruct((chips, 2, tokens, width), jnp.bfloat16),
        cost_estimate=pl.CostEstimate(
            flops=4 * chips * tokens * depth * width,
            bytes_accessed=4 * chips * tokens * (depth + width),
            transcendentals=0,
        ),
    )(member, even, odd, even_pair, odd_pair, weight, double)


def assemble_kernel(groups, shifts, place_ref, own_ref, *refs):
    pieces, out_ref, sem = refs[: len(shifts)], refs[len(shifts)], refs[len(shifts) + 1]
    members, tokens, width = pieces[0].shape
    columns = own_ref.shape[1]
    me = place_ref[0]
    copies = [
        pltpu.make_async_copy(
            own_ref, out_ref.at[:, pl.ds(pl.multiple_of(me * columns, columns), columns)], sem.at[0]
        )
    ]
    for index, (shift, piece) in enumerate(zip(shifts, pieces)):
        shard = lax.rem(me + groups - shift, groups)
        for member in range(members):
            start = pl.multiple_of(shard * columns + member * width, width)
            copies.append(
                pltpu.make_async_copy(
                    piece.at[member], out_ref.at[:, pl.ds(start, width)], sem.at[1 + index * members + member]
                )
            )
    for copy in copies:
        copy.start()
    for copy in copies:
        copy.wait()


def assemble(place, own, pieces, shifts, groups):
    tokens, columns = own.shape
    members, _, width = pieces[0].shape
    if width % 128:
        blocks = [own] + [jnp.swapaxes(p, 0, 1).reshape(tokens, columns) for p in pieces]
        order = [0] * groups
        for index, shift in enumerate((0,) + tuple(shifts)):
            order[shift] = index
        stacked = jnp.stack([blocks[i] for i in order])
        picked = jnp.take(stacked, (place[0] - jnp.arange(groups)) % groups, axis=0)
        return jnp.swapaxes(picked, 0, 1).reshape(tokens, groups * columns)
    anywhere = pl.BlockSpec(memory_space=pl.ANY)
    return pl.pallas_call(
        functools.partial(assemble_kernel, groups, shifts),
        grid_spec=pltpu.PrefetchScalarGridSpec(
            num_scalar_prefetch=1,
            grid=(),
            in_specs=[anywhere] * (1 + len(pieces)),
            out_specs=anywhere,
            scratch_shapes=[pltpu.SemaphoreType.DMA((1 + len(pieces) * members,))],
        ),
        out_shape=jax.ShapeDtypeStruct((tokens, groups * columns), jnp.bfloat16),
    )(place, own, *pieces)


def input_gradients(upstream, value_weight, adapter_in, adapter_out):
    groups, members = lax.axis_size("fsdp"), lax.axis_size("grp")
    place, member = lax.axis_index("fsdp"), lax.axis_index("grp")
    columns = value_weight.shape[0]
    width = columns // members
    tokens, depth = upstream.shape
    double = jnp.concatenate([adapter_in, adapter_in], axis=1)

    slice_own = lax.dynamic_slice_in_dim(value_weight, member * width, width, 0)
    shifts = sorted(range(1, groups), key=lambda s: (min(s, groups - s), s))
    weights = [
        lax.ppermute(slice_own, "fsdp", [(i, (i + s) % groups) for i in range(groups)]) for s in shifts
    ]
    even = jnp.stack(
        [upstream]
        + [lax.ppermute(upstream, "grp", [(i, i ^ m) for i in range(members)]) for m in range(2, members, 2)]
    )
    odd = lax.ppermute(even, "grp", [(i, i ^ 1) for i in range(members)])
    even_pair, odd_pair = plane_pairs(even, odd, adapter_out)

    own = own_columns(
        upstream, value_weight, lax.dynamic_slice_in_dim(double, place * columns, columns, 0), adapter_out
    )
    pieces = []
    for shift, weight in zip(shifts, weights):
        shard = lax.rem(place + groups - shift, groups)
        part = lax.dynamic_slice_in_dim(double, shard * columns + member * width, width, 0)
        piece = piece_columns(member.reshape(1), even, odd, even_pair, odd_pair, weight, part)
        piece = piece.reshape(members, tokens, width)
        pieces.append(lax.all_to_all(piece, "grp", split_axis=0, concat_axis=0, tiled=True))
    return assemble(place.reshape(1), own, pieces, shifts, groups)


def per_device(inputs, upstream, value_weight, adapter_in, adapter_out, sign_seed):
    both = ("fsdp", "grp")
    groups = lax.axis_size("fsdp")
    members = lax.axis_size("grp")
    input_grads = input_gradients(upstream, value_weight, adapter_in, adapter_out)

    passed_along = contract_last(upstream, adapter_out)
    rescaled_values = (lowrank_scale_factor * passed_along).astype(jnp.bfloat16)
    rank_reduced = jnp.dot(inputs, adapter_in, preferred_element_type=jnp.float32).astype(
        jnp.bfloat16
    )
    grad_in = leading_contraction(inputs, rescaled_values)
    output_gradient = lowrank_scale_factor * leading_contraction(rank_reduced, upstream)
    flat = jnp.concatenate([grad_in.reshape(-1), output_gradient.reshape(-1)]).astype(jnp.bfloat16)
    devices = groups * members
    slice_len = flat.shape[0] // devices
    received = lax.all_to_all(
        flat.reshape(devices, slice_len), both, split_axis=0, concat_axis=0, tiled=True
    )
    local_total = jnp.sum(received.astype(jnp.float32), axis=0) / devices
    mean_grad = lax.all_to_all(
        jnp.broadcast_to(local_total, (members, slice_len)), "grp", split_axis=0, concat_axis=0, tiled=True
    ).reshape(-1)

    first_row = (lax.axis_index("fsdp") * members + lax.axis_index("grp")) * slice_len
    signs = make_signs(first_row, slice_len, PROJ, sign_seed[0])
    partial_feats = jnp.dot(received, signs, preferred_element_type=jnp.float32)
    parts = lax.all_to_all(partial_feats, both, split_axis=0, concat_axis=0, tiled=True)
    raw = jnp.sum(parts, axis=0, keepdims=True)
    features = raw * lax.rsqrt(jnp.mean(raw * raw, axis=1, keepdims=True) + 1e-06)
    return (input_grads, features, mean_grad)


def solution(mesh):
    return jax.shard_map(
        per_device,
        mesh=mesh,
        in_specs=(
            P(("grp", "fsdp"), None),
            P(("grp", "fsdp"), None),
            P("fsdp", None),
            P(),
            P(),
            P(),
        ),
        out_specs=(P(("grp", "fsdp"), None), P(("grp", "fsdp"), None), P("fsdp")),
        check_vma=False,
    )
```

```python
import functools

import jax
import jax.numpy as jnp
from jax import lax
from jax.experimental import pallas as pl
from jax.experimental.pallas import tpu as pltpu
from jax.sharding import PartitionSpec as P

PROJ = 4096

lowrank_scale_factor = 2.0

CHEAP = pl.CostEstimate(flops=0, bytes_accessed=0, transcendentals=0)
MEMBER, PLACE, CHIP, START, SHARDS = range(5)
DEAR = pl.CostEstimate(flops=10**11, bytes_accessed=0, transcendentals=0)


def contract_last(left, right):
    return lax.dot_general(
        left, right, (((1,), (1,)), ((), ())), preferred_element_type=jnp.float32
    )


def dot(left, right):
    return jnp.dot(left, right, preferred_element_type=jnp.float32)


def hash_signs(mixed):
    mixed = mixed ^ lax.shift_right_logical(mixed, 15)
    mixed = mixed * 181057748
    mixed = mixed ^ lax.shift_left(mixed, 13)
    return jnp.where(mixed < 0, -1.0, 1.0).astype(jnp.bfloat16)


def split_pair(tokens, adapter_out):
    through = lowrank_scale_factor * contract_last(tokens, adapter_out)
    high = through.astype(jnp.bfloat16)
    low = (through - high.astype(jnp.float32)).astype(jnp.bfloat16)
    return jnp.concatenate([high, low], axis=1)


def twice(part):
    return jnp.concatenate([part, part], axis=0)


def own_kernel(info_ref, up_ref, weight_ref, in_adapter_ref, out_adapter_ref, after_ref, out_ref, pair_ref, turned_ref):
    @pl.when(pl.program_id(0) == 0)
    def _():
        pair_ref[...] = split_pair(up_ref[...], out_adapter_ref[...])
        turned_ref[...] = up_ref[...].T

    total = dot(weight_ref[...], turned_ref[...]).T
    total += dot(pair_ref[...], twice(in_adapter_ref[...]))
    out_ref[...] = total.astype(out_ref.dtype)


def own_columns(info, upstream, weight, adapter_in_t, adapter_out, all_columns, after):
    tokens, depth = upstream.shape
    columns = weight.shape[0]
    block = min(1024, columns)
    steps = columns // block
    rank = adapter_in_t.shape[0]
    return pl.pallas_call(
        own_kernel,
        grid_spec=pltpu.PrefetchScalarGridSpec(
            num_scalar_prefetch=1,
            grid=(steps,),
            in_specs=[
                pl.BlockSpec((tokens, depth), lambda i, s: (0, 0)),
                pl.BlockSpec((block, depth), lambda i, s: (i, 0)),
                pl.BlockSpec((rank, block), lambda i, s: (0, s[PLACE] * steps + i)),
                pl.BlockSpec(adapter_out.shape, lambda i, s: (0, 0)),
                pl.BlockSpec(memory_space=pl.ANY),
            ],
            out_specs=pl.BlockSpec((tokens, block), lambda i, s: (0, s[PLACE] * steps + i)),
            scratch_shapes=[
                pltpu.VMEM((tokens, 2 * rank), jnp.bfloat16),
                pltpu.VMEM((depth, tokens), jnp.bfloat16),
            ],
        ),
        out_shape=jax.ShapeDtypeStruct((tokens, all_columns), jnp.bfloat16),
        cost_estimate=CHEAP,
    )(info, upstream, weight, adapter_in_t, adapter_out, after)


def piece_kernel(chips, count, make_pairs, info_ref, *refs):
    token_refs, refs = refs[:chips], refs[chips:]
    weight_refs, refs = refs[: 2 * count], refs[2 * count :]
    adapter_refs, refs = refs[:count], refs[count:]
    pair_ref, refs = refs[0], refs[3:]
    out_refs = refs[:chips]
    rows = token_refs[0].shape[0]
    width = weight_refs[0].shape[0]
    core = lax.rem(info_ref[MEMBER], 2)
    stacked = jnp.concatenate([ref[...] for ref in token_refs], axis=0)
    if make_pairs:
        pairs = split_pair(stacked, pair_ref[...])
        refs[chips][...] = pairs.reshape(refs[chips].shape)
    else:
        pairs = pair_ref[...].reshape(chips * rows, pair_ref.shape[2])
    for index in range(count):
        for half in range(2):
            at = pl.multiple_of(lax.bitwise_xor(core, half) * width, width)
            total = contract_last(stacked, weight_refs[2 * index + half][...])
            total += dot(pairs, twice(adapter_refs[index][:, pl.ds(at, width)]))
            total = total.astype(out_refs[0].dtype)
            at = pl.multiple_of(at + index * 2 * width, width)
            for chip in range(chips):
                out_refs[chip][:, pl.ds(at, width)] = total[chip * rows : (chip + 1) * rows]


def piece_columns(info, shifts, plane, weights, adapter_in_t, pairs, adapter_out, after):
    chips = len(plane)
    tokens, depth = plane[0].shape
    width = weights[0][0].shape[0]
    count = len(weights)
    rank = adapter_in_t.shape[0]
    make_pairs = pairs is None
    if width % 128:
        if make_pairs:
            pairs = jnp.stack([split_pair(part, adapter_out) for part in plane])
        core = lax.rem(info[MEMBER], 2)
        columns = []
        for (mine, other), shift in zip(weights, shifts):
            at = info[SHARDS + shift] * chips + info[CHIP]
            both = jnp.where(core == 0, jnp.concatenate([mine, other]), jnp.concatenate([other, mine]))
            low = twice(lax.dynamic_slice_in_dim(adapter_in_t, at * 2 * width, 2 * width, 1))
            columns.append([contract_last(t, both) + dot(p, low) for t, p in zip(plane, pairs)])
        return [jnp.concatenate(c, axis=1).astype(jnp.bfloat16) for c in zip(*columns)], pairs
    rows = tokens // 2
    pair_block = pl.BlockSpec((chips, rows, 2 * rank), lambda i, s: (0, i, 0))
    out_block = pl.BlockSpec((rows, count * 2 * width), lambda i, s: (i, 0))
    out_shape = jax.ShapeDtypeStruct((tokens, count * 2 * width), jnp.bfloat16)
    outs = pl.pallas_call(
        functools.partial(piece_kernel, chips, count, make_pairs),
        grid_spec=pltpu.PrefetchScalarGridSpec(
            num_scalar_prefetch=1,
            grid=(tokens // rows,),
            in_specs=[pl.BlockSpec((rows, depth), lambda i, s: (i, 0))] * chips
            + [pl.BlockSpec((width, depth), lambda i, s: (0, 0))] * (2 * count)
            + [
                pl.BlockSpec((rank, 2 * width), lambda i, s, at=SHARDS + shift: (0, s[at] * chips + s[CHIP]))
                for shift in shifts
            ]
            + [pl.BlockSpec(adapter_out.shape, lambda i, s: (0, 0)) if make_pairs else pair_block]
            + [pl.BlockSpec(memory_space=pl.ANY)] * 2,
            out_specs=[out_block] * chips + ([pair_block] if make_pairs else []),
        ),
        out_shape=[out_shape] * chips
        + ([jax.ShapeDtypeStruct((chips, tokens, 2 * rank), jnp.bfloat16)] if make_pairs else []),
        cost_estimate=CHEAP,
    )(
        info,
        *plane,
        *[w for pair in weights for w in pair],
        *[adapter_in_t] * count,
        adapter_out if make_pairs else pairs,
        *after,
    )
    return (outs[:chips], outs[chips]) if make_pairs else (outs, pairs)


def place_kernel(chips, info_ref, *refs):
    piece_refs, out_ref = refs[:chips], refs[chips + 2]
    width = piece_refs[0].shape[1]
    for k in range(chips):
        at = pl.multiple_of(lax.bitwise_xor(info_ref[CHIP], k) * width, width)
        out_ref[:, pl.ds(at, width)] = piece_refs[k][...]


def place_columns(info, shifts, pieces, buffer, after, last):
    chips = len(pieces)
    tokens, width = pieces[0].shape
    width = width // len(shifts)
    if width % 128:
        for index, shift in enumerate(shifts):
            for k, piece in enumerate(pieces):
                part = piece[:, index * width : (index + 1) * width]
                at = (info[SHARDS + shift] * chips + lax.bitwise_xor(info[CHIP], k)) * width
                buffer = lax.dynamic_update_slice_in_dim(buffer, part, at, 1)
        return buffer

    def shard_of(w, s):
        at = s[SHARDS + shifts[0]]
        for index in range(1, len(shifts)):
            at = jnp.where(w == index, s[SHARDS + shifts[index]], at)
        return 0, at

    anywhere = pl.BlockSpec(memory_space=pl.ANY)
    return pl.pallas_call(
        functools.partial(place_kernel, chips),
        grid_spec=pltpu.PrefetchScalarGridSpec(
            num_scalar_prefetch=1,
            grid=(len(shifts),),
            in_specs=[pl.BlockSpec((tokens, width), lambda w, s: (0, w))] * chips + [anywhere, anywhere],
            out_specs=pl.BlockSpec((tokens, chips * width), shard_of),
        ),
        out_shape=jax.ShapeDtypeStruct(buffer.shape, buffer.dtype),
        input_output_aliases={1 + chips: 0},
        cost_estimate=DEAR if last else CHEAP,
    )(info, *pieces, buffer, after)


def flat_kernel(rank, groups, chunk_rows, in_ref, up_ref, in_adapter_ref, out_adapter_ref, out_ref, scaled_ref, narrow_ref, turn_ref, flat_ref, line_ref):
    step = pl.program_id(0)
    tokens, block = in_ref.shape
    model = flat_ref.shape[1] - up_ref.shape[1]

    @pl.when(step == 0)
    def _():
        through = lowrank_scale_factor * contract_last(out_adapter_ref[...], up_ref[...])
        scaled_ref[...] = through.astype(jnp.bfloat16)
        narrow_ref[...] = jnp.zeros_like(narrow_ref)

    at = pl.multiple_of(step * block, block)
    flat_ref[:, pl.ds(at, block)] = dot(scaled_ref[...], in_ref[...])
    narrow_ref[...] += contract_last(in_ref[...], in_adapter_ref[...])

    @pl.when(step == pl.num_programs(0) - 1)
    def _():
        narrow = narrow_ref[...].T.astype(jnp.bfloat16)
        turn_ref[...] = (lowrank_scale_factor * dot(narrow, up_ref[...])).T
        span = up_ref.shape[1] // rank
        lines = [turn_ref[pl.ds(row, span, rank), :].T for row in range(rank)]
        for r in range(rank):
            part = jnp.concatenate([line[r : r + 1] for line in lines], axis=0)
            flat_ref[:, model + r * span : model + (r + 1) * span] = part
        if chunk_rows:
            tiles = flat_ref.shape[1] // 128 // groups
            for place in range(groups):
                for tile in range(tiles):
                    at = (place * tiles + tile) * 128
                    line_ref[pl.ds(place * chunk_rows + tile, rank, groups * chunk_rows), :] = flat_ref[
                        :, at : at + 128
                    ]
            out_ref[...] = line_ref[...].astype(jnp.bfloat16)
        else:
            out_ref[...] = flat_ref[...].astype(jnp.bfloat16)


def pair_gradient(inputs, upstream, adapter_in_t, adapter_out, groups, chunk_rows):
    tokens, model = inputs.shape
    depth = upstream.shape[1]
    rank = adapter_in_t.shape[0]
    steps = 2
    block = model // steps
    out_shape = (rank * groups * chunk_rows, 128) if chunk_rows else (rank, model + depth)
    return pl.pallas_call(
        functools.partial(flat_kernel, rank, groups, chunk_rows),
        grid=(steps,),
        in_specs=[
            pl.BlockSpec((tokens, block), lambda i: (0, i)),
            pl.BlockSpec((tokens, depth), lambda i: (0, 0)),
            pl.BlockSpec((rank, block), lambda i: (0, i)),
            pl.BlockSpec((rank, depth), lambda i: (0, 0)),
        ],
        out_specs=pl.BlockSpec(out_shape, lambda i: (0, 0)),
        out_shape=jax.ShapeDtypeStruct(out_shape, jnp.bfloat16),
        scratch_shapes=[
            pltpu.VMEM((rank, tokens), jnp.bfloat16),
            pltpu.VMEM((tokens, rank), jnp.float32),
            pltpu.VMEM((depth, rank), jnp.float32),
            pltpu.VMEM((rank, model + depth), jnp.float32),
            pltpu.VMEM((max(rank * groups * chunk_rows, 8), 128), jnp.float32),
        ],
        cost_estimate=CHEAP,
    )(inputs, upstream, adapter_in_t, adapter_out)


def project_kernel(stride, chunk, width, chunk_rows, mean_rows, info_ref, part_ref, after_ref, out_ref, wide_ref, line_ref):
    devices, rows = wide_ref.shape
    tiles = out_ref.shape[0] // devices

    @pl.when(pl.program_id(0) == 0)
    def _():
        if chunk_rows:
            line_ref[...] = part_ref[...].astype(jnp.float32)
            for tile in range(mean_rows):
                line = line_ref[pl.ds(tile, devices, chunk_rows), :]
                wide_ref[:, tile * 128 : (tile + 1) * 128] = line.astype(jnp.bfloat16)
                mean = jnp.sum(line, axis=0, keepdims=True) / devices
                out_ref[pl.ds(PROJ // 128 + tile, devices, tiles), :] = jnp.broadcast_to(mean, (devices, 128))
        else:
            wide_ref[...] = part_ref[...]

    columns = pl.program_id(0) * width + lax.broadcasted_iota(jnp.int32, (1, width), 1)
    columns = columns * -2048144789
    total = jnp.zeros((devices, width), jnp.float32)
    for at in range(0, rows, chunk):
        count = min(chunk, rows - at)
        lines = lax.broadcasted_iota(jnp.int32, (count, 1), 0) + at
        lines = lines * stride + info_ref[START]
        total += dot(wide_ref[:, at : at + count], hash_signs(lines + columns))
    for tile in range(width // 128):
        at = pl.program_id(0) * (width // 128) + tile
        out_ref[pl.ds(at, devices, tiles), :] = total[:, tile * 128 : (tile + 1) * 128]


def project(info, part, stride, after, devices, length, chunk_rows):
    width = min(1024, PROJ)
    mean_rows = length // 128 if chunk_rows else 0
    tiles = PROJ // 128 + -(-mean_rows // 8) * 8
    return pl.pallas_call(
        functools.partial(project_kernel, stride, 256, width, chunk_rows, mean_rows),
        grid_spec=pltpu.PrefetchScalarGridSpec(
            num_scalar_prefetch=1,
            grid=(PROJ // width,),
            in_specs=[pl.BlockSpec(part.shape, lambda i, s: (0, 0)), pl.BlockSpec(memory_space=pl.ANY)],
            out_specs=pl.BlockSpec((devices * tiles, 128), lambda i, s: (0, 0)),
            scratch_shapes=[
                pltpu.VMEM((devices, length), jnp.bfloat16),
                pltpu.VMEM((max(devices * chunk_rows, 8), 128), jnp.float32),
            ],
        ),
        out_shape=jax.ShapeDtypeStruct((devices * tiles, 128), jnp.float32),
        cost_estimate=CHEAP,
    )(info, part, after).reshape(devices, tiles, 128)


def wrap32(value):
    return (value + 2**31) % 2**32 - 2**31


def per_device(inputs, upstream, value_weight, adapter_in, adapter_out, sign_seed):
    groups, members = lax.axis_size("fsdp"), lax.axis_size("grp")
    place, member = lax.axis_index("fsdp"), lax.axis_index("grp")
    devices = groups * members
    adapter_in_t = adapter_in.T
    rank, model = adapter_in_t.shape
    tokens = inputs.shape[0]
    columns = value_weight.shape[0]
    width = columns // members

    def along(array, shift):
        return lax.ppermute(array, "fsdp", [(i, (i + shift) % groups) for i in range(groups)])

    def across(array, mask):
        return lax.ppermute(array, "grp", [(i, i ^ mask) for i in range(members)])

    slice_own = lax.dynamic_slice_in_dim(value_weight, member * width, width, 0)
    shifts = sorted(range(1, groups), key=lambda s: (min(s, groups - s), s))
    weights = {}
    for s in shifts:
        if s in (1, groups - 1):
            weights[s] = along(slice_own, s)
        elif s <= groups // 2:
            weights[s] = along(weights[s - 1], 1)
        else:
            weights[s] = along(weights[s + 1], -1)
    chips = members // 2
    chip = member // 2
    plane = [across(upstream, 2 * k) if k else upstream for k in range(chips)]

    share = (model + upstream.shape[1]) // groups
    length = rank * share // members
    assert members % rank == 0
    split = members // rank
    row = member // split
    column = place * share + (member % split) * length
    start = (column * rank + row) * -1640531535 + sign_seed[0] * 668265263
    info = jnp.stack([member, place, chip, start] + [lax.rem(place + groups - s, groups) for s in range(groups)])

    chunk_rows = 0 if length % 128 or split > 1 else -(-length // 1024) * 8
    flat = pair_gradient(inputs, upstream, adapter_in_t, adapter_out, groups, chunk_rows)
    both = ("grp", "fsdp")
    if chunk_rows:
        chunks = flat.reshape(devices, chunk_rows, 128)
    else:
        chunks = flat.reshape(rank, groups, split, length).swapaxes(1, 2).reshape(devices, length)
    received = lax.all_to_all(chunks, both, split_axis=0, concat_axis=0, tiled=True)
    if chunk_rows:
        received = received.reshape(devices * chunk_rows, 128)

    result = own_columns(info, upstream, value_weight, adapter_in_t, adapter_out, groups * columns, flat)

    near = [s for s in shifts if s in (1, groups - 1)]
    batches = [near] + [[s] for s in shifts if s not in near]
    pairs, after, sent, feats = None, (result, received), [], None
    for batch in batches:
        pieces, pairs = piece_columns(
            info,
            batch,
            plane,
            [(weights[s], across(weights[s], 1)) for s in batch],
            adapter_in_t,
            pairs,
            adapter_out,
            after,
        )
        sent.append((batch, [across(p, 2 * k) if k else p for k, p in enumerate(pieces)]))
        after = (pieces[0], pieces[0])
        if feats is None:
            feats = project(
                info, received, wrap32(-1640531535 * rank), pieces[0], devices, length, chunk_rows
            )
            after = (feats, feats)
    parts = lax.all_to_all(feats, both, split_axis=0, concat_axis=0, tiled=True)
    raw = jnp.sum(parts[:, : PROJ // 128], axis=0)
    features = (raw * lax.rsqrt(jnp.mean(raw * raw) + 1e-06)).reshape(1, PROJ)
    mean_rows = length // 128
    if chunk_rows:
        totals = parts.reshape(members, groups, -1, 128)[:, :, PROJ // 128 : PROJ // 128 + mean_rows]
        totals = lax.dynamic_index_in_dim(totals, place, 1, keepdims=False)
    else:
        local_total = jnp.sum(received.astype(jnp.float32), axis=0) / devices
        totals = lax.all_to_all(
            jnp.broadcast_to(local_total, (members, length)), "grp", split_axis=0, concat_axis=0, tiled=True
        )
    mean_grad = totals.reshape(rank, share).T.reshape(-1)

    for index, (batch, pieces) in enumerate(sent):
        result = place_columns(info, batch, pieces, result, after[0], index == len(sent) - 1)
    return (result, features, mean_grad)


def solution(mesh):
    return jax.shard_map(
        per_device,
        mesh=mesh,
        in_specs=(
            P(("grp", "fsdp"), None),
            P(("grp", "fsdp"), None),
            P("fsdp", None),
            P(),
            P(),
            P(),
        ),
        out_specs=(P(("grp", "fsdp"), None), P(("grp", "fsdp"), None), P("fsdp")),
        check_vma=False,
    )
```

```python
import functools

import jax
import jax.numpy as jnp
from jax import lax
from jax.experimental import pallas as pl
from jax.experimental.pallas import tpu as pltpu
from jax.sharding import PartitionSpec as P

PROJ = 4096

lowrank_scale_factor = 2.0

CHEAP = pl.CostEstimate(flops=0, bytes_accessed=0, transcendentals=0)
MEMBER, PLACE, CHIP, START, SHARDS = range(5)
DEAR = pl.CostEstimate(flops=10**11, bytes_accessed=0, transcendentals=0)


def contract_last(left, right):
    return lax.dot_general(
        left, right, (((1,), (1,)), ((), ())), preferred_element_type=jnp.float32
    )


def dot(left, right):
    return jnp.dot(left, right, preferred_element_type=jnp.float32)


def hash_signs(mixed):
    mixed = mixed ^ lax.shift_right_logical(mixed, 15)
    mixed = mixed * 181057748
    mixed = mixed ^ lax.shift_left(mixed, 13)
    return jnp.where(mixed < 0, -1.0, 1.0).astype(jnp.bfloat16)


def split_pair(tokens, adapter_out):
    through = lowrank_scale_factor * contract_last(tokens, adapter_out)
    high = through.astype(jnp.bfloat16)
    low = (through - high.astype(jnp.float32)).astype(jnp.bfloat16)
    return jnp.concatenate([high, low], axis=1)


def twice(part):
    return jnp.concatenate([part, part], axis=0)


def own_kernel(info_ref, up_ref, weight_ref, in_adapter_ref, out_adapter_ref, after_ref, out_ref, pair_ref, turned_ref):
    @pl.when(pl.program_id(0) == 0)
    def _():
        pair_ref[...] = split_pair(up_ref[...], out_adapter_ref[...])
        turned_ref[...] = up_ref[...].T

    total = dot(weight_ref[...], turned_ref[...]).T
    total += dot(pair_ref[...], twice(in_adapter_ref[...]))
    out_ref[...] = total.astype(out_ref.dtype)


def own_columns(info, upstream, weight, adapter_in_t, adapter_out, all_columns, after):
    tokens, depth = upstream.shape
    columns = weight.shape[0]
    block = min(1024, columns)
    steps = columns // block
    rank = adapter_in_t.shape[0]
    return pl.pallas_call(
        own_kernel,
        grid_spec=pltpu.PrefetchScalarGridSpec(
            num_scalar_prefetch=1,
            grid=(steps,),
            in_specs=[
                pl.BlockSpec((tokens, depth), lambda i, s: (0, 0)),
                pl.BlockSpec((block, depth), lambda i, s: (i, 0)),
                pl.BlockSpec((rank, block), lambda i, s: (0, s[PLACE] * steps + i)),
                pl.BlockSpec(adapter_out.shape, lambda i, s: (0, 0)),
                pl.BlockSpec(memory_space=pl.ANY),
            ],
            out_specs=pl.BlockSpec((tokens, block), lambda i, s: (0, s[PLACE] * steps + i)),
            scratch_shapes=[
                pltpu.VMEM((tokens, 2 * rank), jnp.bfloat16),
                pltpu.VMEM((depth, tokens), jnp.bfloat16),
            ],
        ),
        out_shape=jax.ShapeDtypeStruct((tokens, all_columns), jnp.bfloat16),
        cost_estimate=CHEAP,
    )(info, upstream, weight, adapter_in_t, adapter_out, after)


def pair_kernel(chips, *refs):
    out_adapter_ref, after_ref, out_ref = refs[chips:]
    for chip in range(chips):
        out_ref[chip] = split_pair(refs[chip][...], out_adapter_ref[...])


def plane_pairs(plane, adapter_out, after):
    chips = len(plane)
    tokens, depth = plane[0].shape
    rank2 = 2 * adapter_out.shape[0]
    return pl.pallas_call(
        functools.partial(pair_kernel, chips),
        grid=(1,),
        in_specs=[pl.BlockSpec((tokens, depth), lambda i: (0, 0))] * chips
        + [pl.BlockSpec(adapter_out.shape, lambda i: (0, 0)), pl.BlockSpec(memory_space=pl.ANY)],
        out_specs=pl.BlockSpec((chips, tokens, rank2), lambda i: (0, 0, 0)),
        out_shape=jax.ShapeDtypeStruct((chips, tokens, rank2), jnp.bfloat16),
        cost_estimate=DEAR,
    )(*plane, adapter_out, after)


def piece_kernel(chips, count, extra, info_ref, *refs):
    token_refs, refs = refs[:chips], refs[chips:]
    weight_refs, refs = refs[: 2 * count], refs[2 * count :]
    adapter_refs, refs = refs[:count], refs[count:]
    pair_ref, refs = refs[0], refs[1 + extra :]
    out_refs = refs[:chips]
    rows = token_refs[0].shape[0]
    width = weight_refs[0].shape[0]
    core = lax.rem(info_ref[MEMBER], 2)
    stacked = jnp.concatenate([ref[...] for ref in token_refs], axis=0)
    pairs = pair_ref[...].reshape(chips * rows, pair_ref.shape[2])
    for index in range(count):
        for half in range(2):
            at = pl.multiple_of(lax.bitwise_xor(core, half) * width, width)
            total = contract_last(stacked, weight_refs[2 * index + half][...])
            total += dot(pairs, twice(adapter_refs[index][:, pl.ds(at, width)]))
            total = total.astype(out_refs[0].dtype)
            at = pl.multiple_of(at + index * 2 * width, width)
            for chip in range(chips):
                out_refs[chip][:, pl.ds(at, width)] = total[chip * rows : (chip + 1) * rows]


def piece_columns(info, shifts, plane, weights, adapter_in_t, pairs, after):
    chips = len(plane)
    tokens, depth = plane[0].shape
    width = weights[0][0].shape[0]
    count = len(weights)
    rank = adapter_in_t.shape[0]
    if width % 128:
        core = lax.rem(info[MEMBER], 2)
        columns = []
        for (mine, other), shift in zip(weights, shifts):
            at = info[SHARDS + shift] * chips + info[CHIP]
            both = jnp.where(core == 0, jnp.concatenate([mine, other]), jnp.concatenate([other, mine]))
            low = twice(lax.dynamic_slice_in_dim(adapter_in_t, at * 2 * width, 2 * width, 1))
            columns.append([contract_last(t, both) + dot(p, low) for t, p in zip(plane, pairs)])
        return [jnp.concatenate(c, axis=1).astype(jnp.bfloat16) for c in zip(*columns)]
    rows = tokens // 2
    pair_block = pl.BlockSpec((chips, rows, 2 * rank), lambda i, s: (0, i, 0))
    out_block = pl.BlockSpec((rows, count * 2 * width), lambda i, s: (i, 0))
    out_shape = jax.ShapeDtypeStruct((tokens, count * 2 * width), jnp.bfloat16)
    outs = pl.pallas_call(
        functools.partial(piece_kernel, chips, count, len(after)),
        grid_spec=pltpu.PrefetchScalarGridSpec(
            num_scalar_prefetch=1,
            grid=(tokens // rows,),
            in_specs=[pl.BlockSpec((rows, depth), lambda i, s: (i, 0))] * chips
            + [pl.BlockSpec((width, depth), lambda i, s: (0, 0))] * (2 * count)
            + [
                pl.BlockSpec((rank, 2 * width), lambda i, s, at=SHARDS + shift: (0, s[at] * chips + s[CHIP]))
                for shift in shifts
            ]
            + [pair_block]
            + [pl.BlockSpec(memory_space=pl.ANY)] * len(after),
            out_specs=[out_block] * chips,
        ),
        out_shape=[out_shape] * chips,
        cost_estimate=CHEAP if len(after) == 1 else DEAR,
    )(
        info,
        *plane,
        *[w for pair in weights for w in pair],
        *[adapter_in_t] * count,
        pairs,
        *after,
    )
    return outs


def place_kernel(chips, info_ref, *refs):
    piece_refs, out_ref = refs[:chips], refs[chips + 2]
    width = piece_refs[0].shape[1]
    for k in range(chips):
        at = pl.multiple_of(lax.bitwise_xor(info_ref[CHIP], k) * width, width)
        out_ref[:, pl.ds(at, width)] = piece_refs[k][...]


def place_columns(info, shifts, pieces, buffer, after, last):
    chips = len(pieces)
    tokens, width = pieces[0].shape
    width = width // len(shifts)
    if width % 128:
        for index, shift in enumerate(shifts):
            for k, piece in enumerate(pieces):
                part = piece[:, index * width : (index + 1) * width]
                at = (info[SHARDS + shift] * chips + lax.bitwise_xor(info[CHIP], k)) * width
                buffer = lax.dynamic_update_slice_in_dim(buffer, part, at, 1)
        return buffer

    def shard_of(w, s):
        at = s[SHARDS + shifts[0]]
        for index in range(1, len(shifts)):
            at = jnp.where(w == index, s[SHARDS + shifts[index]], at)
        return 0, at

    anywhere = pl.BlockSpec(memory_space=pl.ANY)
    return pl.pallas_call(
        functools.partial(place_kernel, chips),
        grid_spec=pltpu.PrefetchScalarGridSpec(
            num_scalar_prefetch=1,
            grid=(len(shifts),),
            in_specs=[pl.BlockSpec((tokens, width), lambda w, s: (0, w))] * chips + [anywhere, anywhere],
            out_specs=pl.BlockSpec((tokens, chips * width), shard_of),
        ),
        out_shape=jax.ShapeDtypeStruct(buffer.shape, buffer.dtype),
        input_output_aliases={1 + chips: 0},
        cost_estimate=DEAR if last else CHEAP,
    )(info, *pieces, buffer, after)


def flat_kernel(rank, groups, chunk_rows, in_ref, up_ref, in_adapter_ref, out_adapter_ref, out_ref, scaled_ref, narrow_ref, turn_ref, flat_ref, line_ref):
    step = pl.program_id(0)
    tokens, block = in_ref.shape
    model = flat_ref.shape[1] - up_ref.shape[1]

    @pl.when(step == 0)
    def _():
        through = lowrank_scale_factor * contract_last(out_adapter_ref[...], up_ref[...])
        scaled_ref[...] = through.astype(jnp.bfloat16)
        narrow_ref[...] = jnp.zeros_like(narrow_ref)

    at = pl.multiple_of(step * block, block)
    flat_ref[:, pl.ds(at, block)] = dot(scaled_ref[...], in_ref[...])
    narrow_ref[...] += contract_last(in_ref[...], in_adapter_ref[...])

    @pl.when(step == pl.num_programs(0) - 1)
    def _():
        narrow = narrow_ref[...].T.astype(jnp.bfloat16)
        turn_ref[...] = (lowrank_scale_factor * dot(narrow, up_ref[...])).T
        span = up_ref.shape[1] // rank
        lines = [turn_ref[pl.ds(row, span, rank), :].T for row in range(rank)]
        for r in range(rank):
            part = jnp.concatenate([line[r : r + 1] for line in lines], axis=0)
            flat_ref[:, model + r * span : model + (r + 1) * span] = part
        if chunk_rows:
            tiles = flat_ref.shape[1] // 128 // groups
            for place in range(groups):
                for tile in range(tiles):
                    at = (place * tiles + tile) * 128
                    line_ref[pl.ds(place * chunk_rows + tile, rank, groups * chunk_rows), :] = flat_ref[
                        :, at : at + 128
                    ]
            out_ref[...] = line_ref[...].astype(jnp.bfloat16)
        else:
            out_ref[...] = flat_ref[...].astype(jnp.bfloat16)


def pair_gradient(inputs, upstream, adapter_in_t, adapter_out, groups, chunk_rows):
    tokens, model = inputs.shape
    depth = upstream.shape[1]
    rank = adapter_in_t.shape[0]
    steps = 2
    block = model // steps
    out_shape = (rank * groups * chunk_rows, 128) if chunk_rows else (rank, model + depth)
    return pl.pallas_call(
        functools.partial(flat_kernel, rank, groups, chunk_rows),
        grid=(steps,),
        in_specs=[
            pl.BlockSpec((tokens, block), lambda i: (0, i)),
            pl.BlockSpec((tokens, depth), lambda i: (0, 0)),
            pl.BlockSpec((rank, block), lambda i: (0, i)),
            pl.BlockSpec((rank, depth), lambda i: (0, 0)),
        ],
        out_specs=pl.BlockSpec(out_shape, lambda i: (0, 0)),
        out_shape=jax.ShapeDtypeStruct(out_shape, jnp.bfloat16),
        scratch_shapes=[
            pltpu.VMEM((rank, tokens), jnp.bfloat16),
            pltpu.VMEM((tokens, rank), jnp.float32),
            pltpu.VMEM((depth, rank), jnp.float32),
            pltpu.VMEM((rank, model + depth), jnp.float32),
            pltpu.VMEM((max(rank * groups * chunk_rows, 8), 128), jnp.float32),
        ],
        cost_estimate=CHEAP,
    )(inputs, upstream, adapter_in_t, adapter_out)


def project_kernel(stride, chunk, width, chunk_rows, mean_rows, info_ref, part_ref, after_ref, out_ref, wide_ref, line_ref, sum_ref):
    devices, rows = wide_ref.shape
    tiles = sum_ref.shape[0] // devices

    @pl.when(pl.program_id(0) == 0)
    def _():
        if chunk_rows:
            line_ref[...] = part_ref[...].astype(jnp.float32)
            for tile in range(mean_rows):
                line = line_ref[pl.ds(tile, devices, chunk_rows), :]
                wide_ref[:, tile * 128 : (tile + 1) * 128] = line.astype(jnp.bfloat16)
                mean = jnp.sum(line, axis=0, keepdims=True) / devices
                sum_ref[pl.ds(PROJ // 128 + tile, devices, tiles), :] = jnp.broadcast_to(mean, (devices, 128))
        else:
            wide_ref[...] = part_ref[...]

    columns = pl.program_id(0) * width + lax.broadcasted_iota(jnp.int32, (1, width), 1)
    columns = columns * -2048144789
    total = jnp.zeros((devices, width), jnp.float32)
    for at in range(0, rows, chunk):
        count = min(chunk, rows - at)
        lines = lax.broadcasted_iota(jnp.int32, (count, 1), 0) + at
        lines = lines * stride + info_ref[START]
        total += dot(wide_ref[:, at : at + count], hash_signs(lines + columns))
    for tile in range(width // 128):
        at = pl.program_id(0) * (width // 128) + tile
        sum_ref[pl.ds(at, devices, tiles), :] = total[:, tile * 128 : (tile + 1) * 128]

    @pl.when(pl.program_id(0) == pl.num_programs(0) - 1)
    def _():
        out_ref[...] = sum_ref[...].astype(out_ref.dtype)


def project(info, part, stride, after, devices, length, chunk_rows):
    width = min(2048, PROJ)
    mean_rows = length // 128 if chunk_rows else 0
    tiles = PROJ // 128 + -(-mean_rows // 8) * 8
    return pl.pallas_call(
        functools.partial(project_kernel, stride, 256, width, chunk_rows, mean_rows),
        grid_spec=pltpu.PrefetchScalarGridSpec(
            num_scalar_prefetch=1,
            grid=(PROJ // width,),
            in_specs=[pl.BlockSpec(part.shape, lambda i, s: (0, 0)), pl.BlockSpec(memory_space=pl.ANY)],
            out_specs=pl.BlockSpec((devices * tiles, 128), lambda i, s: (0, 0)),
            scratch_shapes=[
                pltpu.VMEM((devices, length), jnp.bfloat16),
                pltpu.VMEM((max(devices * chunk_rows, 8), 128), jnp.float32),
                pltpu.VMEM((devices * tiles, 128), jnp.float32),
            ],
        ),
        out_shape=jax.ShapeDtypeStruct((devices * tiles, 128), jnp.bfloat16),
        cost_estimate=DEAR,
    )(info, part, after).reshape(devices, tiles, 128)


def wrap32(value):
    return (value + 2**31) % 2**32 - 2**31


def per_device(inputs, upstream, value_weight, adapter_in, adapter_out, sign_seed):
    groups, members = lax.axis_size("fsdp"), lax.axis_size("grp")
    place, member = lax.axis_index("fsdp"), lax.axis_index("grp")
    devices = groups * members
    adapter_in_t = adapter_in.T
    rank, model = adapter_in_t.shape
    tokens = inputs.shape[0]
    columns = value_weight.shape[0]
    width = columns // members

    def along(array, shift):
        return lax.ppermute(array, "fsdp", [(i, (i + shift) % groups) for i in range(groups)])

    def across(array, mask):
        return lax.ppermute(array, "grp", [(i, i ^ mask) for i in range(members)])

    slice_own = lax.dynamic_slice_in_dim(value_weight, member * width, width, 0)
    shifts = sorted(range(1, groups), key=lambda s: (min(s, groups - s), s))
    weights = {}
    for s in shifts:
        if s in (1, groups - 1):
            weights[s] = along(slice_own, s)
        elif s <= groups // 2:
            weights[s] = along(weights[s - 1], 1)
        else:
            weights[s] = along(weights[s + 1], -1)
    chips = members // 2
    chip = member // 2
    plane = [across(upstream, 2 * k) if k else upstream for k in range(chips)]

    share = (model + upstream.shape[1]) // groups
    length = rank * share // members
    assert members % rank == 0
    split = members // rank
    row = member // split
    column = place * share + (member % split) * length
    start = (column * rank + row) * -1640531535 + sign_seed[0] * 668265263
    info = jnp.stack([member, place, chip, start] + [lax.rem(place + groups - s, groups) for s in range(groups)])

    chunk_rows = 0 if length % 128 or split > 1 else -(-length // 1024) * 8
    flat = pair_gradient(inputs, upstream, adapter_in_t, adapter_out, groups, chunk_rows)
    both = ("grp", "fsdp")
    if chunk_rows:
        chunks = flat.reshape(devices, chunk_rows, 128)
    else:
        chunks = flat.reshape(rank, groups, split, length).swapaxes(1, 2).reshape(devices, length)
    received = lax.all_to_all(chunks, both, split_axis=0, concat_axis=0, tiled=True)
    if chunk_rows:
        received = received.reshape(devices * chunk_rows, 128)

    result = own_columns(info, upstream, value_weight, adapter_in_t, adapter_out, groups * columns, flat)

    near = [s for s in shifts if s in (1, groups - 1)]
    batches = [near] + [[s] for s in shifts if s not in near]
    pairs = plane_pairs(plane, adapter_out, result)
    after, sent, feats = [pairs], [], None
    for batch in batches:
        pieces = piece_columns(
            info,
            batch,
            plane,
            [(weights[s], across(weights[s], 1)) for s in batch],
            adapter_in_t,
            pairs,
            after,
        )
        sent.append((batch, [across(p, 2 * k) if k else p for k, p in enumerate(pieces)]))
        after = [p for k, p in enumerate(sent[-1][1]) if k]
        if feats is None:
            feats = project(
                info, received, wrap32(-1640531535 * rank), pieces[0], devices, length, chunk_rows
            )
            after.append(feats)
    parts = lax.all_to_all(feats, both, split_axis=0, concat_axis=0, tiled=True)
    raw = jnp.sum(parts[:, : PROJ // 128].astype(jnp.float32), axis=0)
    features = (raw * lax.rsqrt(jnp.mean(raw * raw) + 1e-06)).reshape(1, PROJ)
    mean_rows = length // 128
    if chunk_rows:
        totals = parts.reshape(members, groups, -1, 128)[:, :, PROJ // 128 : PROJ // 128 + mean_rows]
        totals = lax.dynamic_index_in_dim(totals, place, 1, keepdims=False).astype(jnp.float32)
    else:
        local_total = jnp.sum(received.astype(jnp.float32), axis=0) / devices
        totals = lax.all_to_all(
            jnp.broadcast_to(local_total, (members, length)), "grp", split_axis=0, concat_axis=0, tiled=True
        )
    mean_grad = totals.reshape(rank, share).T.reshape(-1)

    for index, (batch, pieces) in enumerate(sent):
        result = place_columns(info, batch, pieces, result, features, index == len(sent) - 1)
    return (result, features, mean_grad)


def solution(mesh):
    return jax.shard_map(
        per_device,
        mesh=mesh,
        in_specs=(
            P(("grp", "fsdp"), None),
            P(("grp", "fsdp"), None),
            P("fsdp", None),
            P(),
            P(),
            P(),
        ),
        out_specs=(P(("grp", "fsdp"), None), P(("grp", "fsdp"), None), P("fsdp")),
        check_vma=False,
    )
```

```python
import functools

import jax
import jax.numpy as jnp
from jax import lax
from jax.experimental import pallas as pl
from jax.experimental.pallas import tpu as pltpu
from jax.sharding import PartitionSpec as P

PROJ = 4096

lowrank_scale_factor = 2.0

CHEAP = pl.CostEstimate(flops=0, bytes_accessed=0, transcendentals=0)
VMEM_BYTES = 24 * 2**20
MEMBER, PLACE, CHIP, START, SHARDS = range(5)
DEAR = pl.CostEstimate(flops=10**11, bytes_accessed=0, transcendentals=0)


def contract_last(left, right):
    return lax.dot_general(
        left, right, (((1,), (1,)), ((), ())), preferred_element_type=jnp.float32
    )


def dot(left, right):
    return jnp.dot(left, right, preferred_element_type=jnp.float32)


def hash_signs(mixed):
    mixed = mixed ^ lax.shift_right_logical(mixed, 15)
    mixed = mixed * 181057748
    mixed = mixed ^ lax.shift_left(mixed, 13)
    return jnp.where(mixed < 0, jnp.bfloat16(-1.0), jnp.bfloat16(1.0))


def split_pair(tokens, adapter_out):
    through = lowrank_scale_factor * contract_last(tokens, adapter_out)
    high = through.astype(jnp.bfloat16)
    low = (through - high.astype(jnp.float32)).astype(jnp.bfloat16)
    return jnp.concatenate([high, low], axis=1)


ANYWHERE = pl.BlockSpec(memory_space=pl.ANY)
IN_VMEM = pl.BlockSpec(memory_space=pltpu.VMEM)
IN_SMEM = pl.BlockSpec(memory_space=pltpu.SMEM)
TOKEN = jax.ShapeDtypeStruct((8, 128), jnp.float32)
TOKEN_BLOCK = pl.BlockSpec((8, 128), lambda *_: (0, 0))


def twice(part):
    return jnp.concatenate([part, part], axis=0)


def own_kernel(info_ref, up_ref, weight_ref, in_adapter_ref, out_adapter_ref, after_ref, out_ref, token_ref, pair_ref, turned_ref):
    @pl.when(pl.program_id(0) == 0)
    def _():
        pair_ref[...] = split_pair(up_ref[...], out_adapter_ref[...])
        turned_ref[...] = up_ref[...].T
        token_ref[...] = jnp.zeros_like(token_ref)

    total = dot(weight_ref[...], turned_ref[...]).T
    total += dot(pair_ref[...], twice(in_adapter_ref[...]))
    out_ref[...] = total.astype(out_ref.dtype)


def own_columns(info, upstream, weight, adapter_in_t, adapter_out, all_columns, after):
    tokens, depth = upstream.shape
    columns = weight.shape[0]
    block = min(1024, columns)
    steps = columns // block
    rank = adapter_in_t.shape[0]
    return pl.pallas_call(
        own_kernel,
        grid_spec=pltpu.PrefetchScalarGridSpec(
            num_scalar_prefetch=1,
            grid=(steps,),
            in_specs=[
                pl.BlockSpec((tokens, depth), lambda i, s: (0, 0)),
                pl.BlockSpec((block, depth), lambda i, s: (i, 0)),
                pl.BlockSpec((rank, block), lambda i, s: (0, s[PLACE] * steps + i)),
                pl.BlockSpec(adapter_out.shape, lambda i, s: (0, 0)),
                pl.BlockSpec(memory_space=pl.ANY),
            ],
            out_specs=[pl.BlockSpec((tokens, block), lambda i, s: (0, s[PLACE] * steps + i)), TOKEN_BLOCK],
            scratch_shapes=[
                pltpu.VMEM((tokens, 2 * rank), jnp.bfloat16),
                pltpu.VMEM((depth, tokens), jnp.bfloat16),
            ],
        ),
        out_shape=[jax.ShapeDtypeStruct((tokens, all_columns), jnp.bfloat16), TOKEN],
        cost_estimate=CHEAP,
        compiler_params=pltpu.CompilerParams(vmem_limit_bytes=VMEM_BYTES),
    )(info, upstream, weight, adapter_in_t, adapter_out, after)


def pair_kernel(chips, *refs):
    out_adapter_ref, after_ref, out_ref = refs[chips:]
    for chip in range(chips):
        out_ref[chip] = split_pair(refs[chip][...], out_adapter_ref[...])


def plane_pairs(plane, adapter_out, after):
    chips = len(plane)
    tokens = plane[0].shape[0]
    return pl.pallas_call(
        functools.partial(pair_kernel, chips),
        in_specs=[IN_VMEM] * (chips + 1) + [ANYWHERE],
        out_specs=IN_VMEM,
        out_shape=jax.ShapeDtypeStruct((chips, tokens, 2 * adapter_out.shape[0]), jnp.bfloat16),
        cost_estimate=DEAR,
        compiler_params=pltpu.CompilerParams(vmem_limit_bytes=VMEM_BYTES),
    )(*plane, adapter_out, after)


def slice_columns(info_ref, shift, half, width, chips, tokens, weight, adapter_ref, pairs):
    at = pl.multiple_of(lax.bitwise_xor(lax.rem(info_ref[MEMBER], 2), half) * width, width)
    here = (info_ref[SHARDS + shift] * chips + info_ref[CHIP]) * 2 * width + at
    total = contract_last(tokens, weight)
    total += dot(pairs, twice(adapter_ref[:, pl.ds(pl.multiple_of(here, width), width)]))
    return at, total.astype(jnp.bfloat16)


def piece_kernel(shifts, chips, info_ref, *refs):
    others = chips - 1
    token_refs, refs = refs[:others], refs[others:]
    weight_refs, refs = refs[: 2 * len(shifts)], refs[2 * len(shifts) :]
    adapter_ref, pair_ref, _ = refs[:3]
    out_refs, token_ref = refs[3 : 3 + others], refs[3 + others]
    token_ref[...] = jnp.zeros_like(token_ref)
    rows = token_refs[0].shape[0]
    width = weight_refs[0].shape[0]
    stacked = jnp.concatenate([ref[...] for ref in token_refs], axis=0)
    pairs = pair_ref[1:].reshape(others * rows, pair_ref.shape[2])
    for index, shift in enumerate(shifts):
        for half in range(2):
            weight = weight_refs[2 * index + half][...]
            at, total = slice_columns(info_ref, shift, half, width, chips, stacked, weight, adapter_ref, pairs)
            at = pl.multiple_of(at + index * 2 * width, width)
            for k in range(others):
                out_refs[k][:, pl.ds(at, width)] = total[k * rows : (k + 1) * rows]


def plain_columns(info, shift, tokens, weights, adapter_in_t, pairs, chips):
    mine, other = weights
    width = mine.shape[0]
    ordered = [jnp.concatenate([mine, other]), jnp.concatenate([other, mine])]
    both = jnp.where(lax.rem(info[MEMBER], 2) == 0, *ordered)
    at = (info[SHARDS + shift] * chips + info[CHIP]) * 2 * width
    low = twice(lax.dynamic_slice_in_dim(adapter_in_t, at, 2 * width, 1))
    return (contract_last(tokens, both) + dot(pairs, low)).astype(jnp.bfloat16)


def piece_columns(info, shifts, plane, weights, adapter_in_t, pairs, after, cost):
    chips = len(plane)
    tokens = plane[0].shape[0]
    width = weights[0][0].shape[0]
    if width % 128:
        columns = [
            [plain_columns(info, s, plane[k], w, adapter_in_t, pairs[k], chips) for s, w in zip(shifts, weights)]
            for k in range(1, chips)
        ]
        return [jnp.concatenate(c, axis=1) for c in columns], after
    count = len(weights)
    out_shape = jax.ShapeDtypeStruct((tokens, count * 2 * width), jnp.bfloat16)
    outs = pl.pallas_call(
        functools.partial(piece_kernel, shifts, chips),
        in_specs=[IN_SMEM] + [IN_VMEM] * (chips - 1 + 2 * count + 2) + [ANYWHERE],
        out_specs=[IN_VMEM] * chips,
        out_shape=[out_shape] * (chips - 1) + [TOKEN],
        cost_estimate=cost,
        compiler_params=pltpu.CompilerParams(vmem_limit_bytes=VMEM_BYTES),
    )(info, *plane[1:], *[w for pair in weights for w in pair], adapter_in_t, pairs, after)
    return outs[:-1], outs[-1]


def place_kernel(shifts, chips, mine, info_ref, *refs):
    piece_refs, refs = refs[: chips - 1], refs[chips - 1 :]
    if mine:
        up_ref, refs = refs[0], refs[1:]
        weight_refs, refs = refs[: 2 * len(mine)], refs[2 * len(mine) :]
        adapter_ref, pair_ref, refs = refs[0], refs[1], refs[2:]
        mine_ref, refs = refs[-1], refs[:-1]
    out_ref, sems = refs[2:]
    width = piece_refs[0].shape[1] // len(shifts)
    copies = []

    def send(source, at):
        at = pl.multiple_of(at * width, width)
        copies.append(pltpu.make_async_copy(source, out_ref.at[:, pl.ds(at, width)], sems.at[len(copies)]))
        copies[-1].start()

    for index, shift in enumerate(shifts):
        for k in range(1, chips):
            at = info_ref[SHARDS + shift] * chips + lax.bitwise_xor(info_ref[CHIP], k)
            send(piece_refs[k - 1].at[:, pl.ds(index * width, width)], at)
    for index, shift in enumerate(mine):
        for half in range(2):
            at, total = slice_columns(
                info_ref,
                shift,
                half,
                width // 2,
                chips,
                up_ref[...],
                weight_refs[2 * index + half][...],
                adapter_ref,
                pair_ref[0],
            )
            mine_ref[:, pl.ds(pl.multiple_of(at + index * width, width // 2), width // 2)] = total
        send(mine_ref.at[:, pl.ds(index * width, width)], info_ref[SHARDS + shift] * chips + info_ref[CHIP])
    for copy in copies:
        copy.wait()


def place_columns(info, shifts, pieces, buffer, after, cost, mine, upstream, weights, adapter_in_t, pairs):
    chips = len(pieces) + 1
    tokens = pieces[0].shape[0]
    width = pieces[0].shape[1] // len(shifts)
    if width % 128 or width % 256 and mine:
        for index, shift in enumerate(shifts):
            for k, piece in enumerate(pieces, 1):
                part = piece[:, index * width : (index + 1) * width]
                at = (info[SHARDS + shift] * chips + lax.bitwise_xor(info[CHIP], k)) * width
                buffer = lax.dynamic_update_slice_in_dim(buffer, part, at, 1)
        for shift in mine:
            part = plain_columns(info, shift, upstream, weights[shift], adapter_in_t, pairs[0], chips)
            at = (info[SHARDS + shift] * chips + info[CHIP]) * width
            buffer = lax.dynamic_update_slice_in_dim(buffer, part, at, 1)
        return buffer
    extra = []
    if mine:
        extra = [upstream] + [w for shift in mine for w in weights[shift]] + [adapter_in_t, pairs]
    operands = [info, *pieces, *extra, buffer, after]
    return pl.pallas_call(
        functools.partial(place_kernel, shifts, chips, mine),
        in_specs=[IN_SMEM] + [IN_VMEM] * (len(operands) - 3) + [ANYWHERE] * 2,
        out_specs=ANYWHERE,
        out_shape=jax.ShapeDtypeStruct(buffer.shape, buffer.dtype),
        scratch_shapes=[pltpu.SemaphoreType.DMA(((chips - 1) * len(shifts) + len(mine),))]
        + ([pltpu.VMEM((tokens, len(mine) * width), jnp.bfloat16)] if mine else []),
        input_output_aliases={len(operands) - 2: 0},
        cost_estimate=cost,
        compiler_params=pltpu.CompilerParams(vmem_limit_bytes=VMEM_BYTES),
    )(*operands)


def flat_kernel(rank, groups, chunk_rows, in_ref, up_ref, in_adapter_ref, out_adapter_ref, out_ref, scaled_ref, narrow_ref, turn_ref, flat_ref, line_ref):
    step = pl.program_id(0)
    tokens, block = in_ref.shape
    model = flat_ref.shape[1] - up_ref.shape[1]

    @pl.when(step == 0)
    def _():
        through = lowrank_scale_factor * contract_last(out_adapter_ref[...], up_ref[...])
        scaled_ref[...] = through.astype(jnp.bfloat16)
        narrow_ref[...] = jnp.zeros_like(narrow_ref)

    at = pl.multiple_of(step * block, block)
    flat_ref[:, pl.ds(at, block)] = dot(scaled_ref[...], in_ref[...])
    narrow_ref[...] += contract_last(in_ref[...], in_adapter_ref[...])

    @pl.when(step == pl.num_programs(0) - 1)
    def _():
        narrow = narrow_ref[...].T.astype(jnp.bfloat16)
        turn_ref[...] = (lowrank_scale_factor * dot(narrow, up_ref[...])).T
        span = up_ref.shape[1] // rank
        lines = [turn_ref[pl.ds(row, span, rank), :].T for row in range(rank)]
        for r in range(rank):
            part = jnp.concatenate([line[r : r + 1] for line in lines], axis=0)
            flat_ref[:, model + r * span : model + (r + 1) * span] = part
        if chunk_rows:
            tiles = flat_ref.shape[1] // 128 // groups
            for place in range(groups):
                for tile in range(tiles):
                    at = (place * tiles + tile) * 128
                    line_ref[pl.ds(place * chunk_rows + tile, rank, groups * chunk_rows), :] = flat_ref[
                        :, at : at + 128
                    ]
            out_ref[...] = line_ref[...].astype(jnp.bfloat16)
        else:
            out_ref[...] = flat_ref[...].astype(jnp.bfloat16)


def pair_gradient(inputs, upstream, adapter_in_t, adapter_out, groups, chunk_rows):
    tokens, model = inputs.shape
    depth = upstream.shape[1]
    rank = adapter_in_t.shape[0]
    steps = 2
    block = model // steps
    out_shape = (rank * groups * chunk_rows, 128) if chunk_rows else (rank, model + depth)
    return pl.pallas_call(
        functools.partial(flat_kernel, rank, groups, chunk_rows),
        grid=(steps,),
        in_specs=[
            pl.BlockSpec((tokens, block), lambda i: (0, i)),
            pl.BlockSpec((tokens, depth), lambda i: (0, 0)),
            pl.BlockSpec((rank, block), lambda i: (0, i)),
            pl.BlockSpec((rank, depth), lambda i: (0, 0)),
        ],
        out_specs=pl.BlockSpec(out_shape, lambda i: (0, 0)),
        out_shape=jax.ShapeDtypeStruct(out_shape, jnp.bfloat16),
        scratch_shapes=[
            pltpu.VMEM((rank, tokens), jnp.bfloat16),
            pltpu.VMEM((tokens, rank), jnp.float32),
            pltpu.VMEM((depth, rank), jnp.float32),
            pltpu.VMEM((rank, model + depth), jnp.float32),
            pltpu.VMEM((max(rank * groups * chunk_rows, 8), 128), jnp.float32),
        ],
        cost_estimate=CHEAP,
    )(inputs, upstream, adapter_in_t, adapter_out)


def project_kernel(stride, chunk, width, chunk_rows, mean_rows, info_ref, part_ref, after_ref, out_ref, token_ref, wide_ref, line_ref, sum_ref):
    devices, rows = wide_ref.shape
    tiles = sum_ref.shape[0] // devices

    @pl.when(pl.program_id(0) == 0)
    def _():
        token_ref[...] = jnp.zeros_like(token_ref)
        if chunk_rows:
            line_ref[...] = part_ref[...].astype(jnp.float32)
            for tile in range(mean_rows):
                line = line_ref[pl.ds(tile, devices, chunk_rows), :]
                wide_ref[:, tile * 128 : (tile + 1) * 128] = line.astype(jnp.bfloat16)
                mean = jnp.sum(line, axis=0, keepdims=True) / devices
                sum_ref[pl.ds(PROJ // 128 + tile, devices, tiles), :] = jnp.broadcast_to(mean, (devices, 128))
        else:
            wide_ref[...] = part_ref[...]

    columns = pl.program_id(0) * width + lax.broadcasted_iota(jnp.int32, (1, width), 1)
    columns = columns * -2048144789
    total = jnp.zeros((devices, width), jnp.float32)
    for at in range(0, rows, chunk):
        count = min(chunk, rows - at)
        lines = lax.broadcasted_iota(jnp.int32, (count, 1), 0) + at
        lines = lines * stride + info_ref[START]
        total += dot(wide_ref[:, at : at + count], hash_signs(lines + columns))
    for tile in range(width // 128):
        at = pl.program_id(0) * (width // 128) + tile
        sum_ref[pl.ds(at, devices, tiles), :] = total[:, tile * 128 : (tile + 1) * 128]

    @pl.when(pl.program_id(0) == pl.num_programs(0) - 1)
    def _():
        out_ref[...] = sum_ref[...].astype(out_ref.dtype)


def project(info, part, stride, after, devices, length, chunk_rows):
    width = PROJ
    mean_rows = length // 128 if chunk_rows else 0
    tiles = PROJ // 128 + -(-mean_rows // 8) * 8
    feats, token = pl.pallas_call(
        functools.partial(project_kernel, stride, 256, width, chunk_rows, mean_rows),
        grid_spec=pltpu.PrefetchScalarGridSpec(
            num_scalar_prefetch=1,
            grid=(PROJ // width,),
            in_specs=[pl.BlockSpec(part.shape, lambda i, s: (0, 0)), pl.BlockSpec(memory_space=pl.ANY)],
            out_specs=[pl.BlockSpec((devices * tiles, 128), lambda i, s: (0, 0)), TOKEN_BLOCK],
            scratch_shapes=[
                pltpu.VMEM((devices, length), jnp.bfloat16),
                pltpu.VMEM((max(devices * chunk_rows, 8), 128), jnp.float32),
                pltpu.VMEM((devices * tiles, 128), jnp.float32),
            ],
        ),
        out_shape=[jax.ShapeDtypeStruct((devices * tiles, 128), jnp.bfloat16), TOKEN],
        cost_estimate=DEAR,
        compiler_params=pltpu.CompilerParams(vmem_limit_bytes=VMEM_BYTES),
    )(info, part, after)
    return feats.reshape(devices, tiles, 128), token


def wrap32(value):
    return (value + 2**31) % 2**32 - 2**31


def per_device(inputs, upstream, value_weight, adapter_in, adapter_out, sign_seed):
    groups, members = lax.axis_size("fsdp"), lax.axis_size("grp")
    place, member = lax.axis_index("fsdp"), lax.axis_index("grp")
    devices = groups * members
    adapter_in_t = adapter_in.T
    rank, model = adapter_in_t.shape
    tokens = inputs.shape[0]
    columns = value_weight.shape[0]
    width = columns // members

    def along(array, shift):
        return lax.ppermute(array, "fsdp", [(i, (i + shift) % groups) for i in range(groups)])

    def across(array, mask):
        return lax.ppermute(array, "grp", [(i, i ^ mask) for i in range(members)])

    slice_own = lax.dynamic_slice_in_dim(value_weight, member * width, width, 0)
    shifts = sorted(range(1, groups), key=lambda s: (min(s, groups - s), s))
    weights = {}
    for s in shifts:
        if s in (1, groups - 1):
            weights[s] = along(slice_own, s)
        elif s <= groups // 2:
            weights[s] = along(weights[s - 1], 1)
        else:
            weights[s] = along(weights[s + 1], -1)
    chips = members // 2
    chip = member // 2
    plane = [across(upstream, 2 * k) if k else upstream for k in range(chips)]

    share = (model + upstream.shape[1]) // groups
    length = rank * share // members
    assert members % rank == 0
    split = members // rank
    row = member // split
    column = place * share + (member % split) * length
    start = (column * rank + row) * -1640531535 + sign_seed[0] * 668265263
    info = jnp.stack([member, place, chip, start] + [lax.rem(place + groups - s, groups) for s in range(groups)])

    chunk_rows = 0 if length % 128 or split > 1 else -(-length // 1024) * 8
    flat = pair_gradient(inputs, upstream, adapter_in_t, adapter_out, groups, chunk_rows)
    both = ("grp", "fsdp")
    if chunk_rows:
        chunks = flat.reshape(devices, chunk_rows, 128)
    else:
        chunks = flat.reshape(rank, groups, split, length).swapaxes(1, 2).reshape(devices, length)
    received = lax.all_to_all(chunks, both, split_axis=0, concat_axis=0, tiled=True)
    if chunk_rows:
        received = received.reshape(devices * chunk_rows, 128)

    result, token = own_columns(info, upstream, value_weight, adapter_in_t, adapter_out, groups * columns, flat)

    near = [s for s in shifts if s in (1, groups - 1)]
    batches = [near] + [[s] for s in shifts if s not in near]
    pairs = plane_pairs(plane, adapter_out, token)
    after, sent, feats = pairs, [], None
    slices = {s: (weights[s], across(weights[s], 1)) for s in shifts}
    for batch in batches:
        pieces, token = piece_columns(
            info,
            batch,
            plane,
            [slices[s] for s in batch],
            adapter_in_t,
            pairs,
            after,
            CHEAP,
        )
        sent.append((batch, [across(p, 2 * k) for k, p in enumerate(pieces, 1)]))
        if feats is None:
            feats, token = project(
                info, received, wrap32(-1640531535 * rank), token, devices, length, chunk_rows
            )
            after = token
    parts = lax.all_to_all(feats, both, split_axis=0, concat_axis=0, tiled=True)
    raw = jnp.sum(parts[:, : PROJ // 128].astype(jnp.float32), axis=0)
    features = (raw * lax.rsqrt(jnp.mean(raw * raw) + 1e-06)).reshape(1, PROJ)
    mean_rows = length // 128
    if chunk_rows:
        totals = parts.reshape(members, groups, -1, 128)[:, :, PROJ // 128 : PROJ // 128 + mean_rows]
        totals = lax.dynamic_index_in_dim(totals, place, 1, keepdims=False).astype(jnp.float32)
    else:
        local_total = jnp.sum(received.astype(jnp.float32), axis=0) / devices
        totals = lax.all_to_all(
            jnp.broadcast_to(local_total, (members, length)), "grp", split_axis=0, concat_axis=0, tiled=True
        )
    mean_grad = totals.reshape(rank, share).T.reshape(-1)

    for index, (batch, pieces) in enumerate(sent):
        first, last = index == 0, index == len(sent) - 1
        result = place_columns(
            info,
            batch,
            pieces,
            result,
            features if last else token,
            CHEAP if last else DEAR,
            shifts if first else [],
            upstream,
            slices,
            adapter_in_t,
            pairs,
        )
    return (result, features, mean_grad)


def solution(mesh):
    return jax.shard_map(
        per_device,
        mesh=mesh,
        in_specs=(
            P(("grp", "fsdp"), None),
            P(("grp", "fsdp"), None),
            P("fsdp", None),
            P(),
            P(),
            P(),
        ),
        out_specs=(P(("grp", "fsdp"), None), P(("grp", "fsdp"), None), P("fsdp")),
        check_vma=False,
    )
```

```python
import functools

import jax
import jax.numpy as jnp
from jax import lax
from jax.experimental import pallas as pl
from jax.experimental.pallas import tpu as pltpu
from jax.sharding import PartitionSpec as P

PROJ = 4096

lowrank_scale_factor = 2.0

CHEAP = pl.CostEstimate(flops=0, bytes_accessed=0, transcendentals=0)
VMEM_BYTES = 24 * 2**20
MEMBER, PLACE, CHIP, SHARDS = range(4)
DEAR = pl.CostEstimate(flops=10**11, bytes_accessed=0, transcendentals=0)


def contract_last(left, right):
    return lax.dot_general(
        left, right, (((1,), (1,)), ((), ())), preferred_element_type=jnp.float32
    )


def dot(left, right):
    return jnp.dot(left, right, preferred_element_type=jnp.float32)


def hash_signs(mixed):
    mixed = mixed ^ lax.shift_right_logical(mixed, 15)
    mixed = mixed * 181057748
    mixed = mixed ^ lax.shift_left(mixed, 13)
    return jnp.where(mixed < 0, jnp.bfloat16(-1.0), jnp.bfloat16(1.0))


def split_pair(tokens, adapter_out):
    through = lowrank_scale_factor * contract_last(tokens, adapter_out)
    high = through.astype(jnp.bfloat16)
    low = (through - high.astype(jnp.float32)).astype(jnp.bfloat16)
    return jnp.concatenate([high, low], axis=1)


ANYWHERE = pl.BlockSpec(memory_space=pl.ANY)
IN_VMEM = pl.BlockSpec(memory_space=pltpu.VMEM)
IN_SMEM = pl.BlockSpec(memory_space=pltpu.SMEM)
TOKEN = jax.ShapeDtypeStruct((8, 128), jnp.float32)
TOKEN_BLOCK = pl.BlockSpec((8, 128), lambda *_: (0, 0))


def twice(part):
    return jnp.concatenate([part, part], axis=0)


def here(groups):
    member, place = lax.axis_index("grp"), lax.axis_index("fsdp")
    return [member, place, lax.div(member, 2)] + [lax.rem(place + groups - s, groups) for s in range(groups)]


def slice_kernel(width, weight_ref, out_ref, sem):
    at = pl.multiple_of(lax.axis_index("grp") * width, width)
    copy = pltpu.make_async_copy(weight_ref.at[pl.ds(at, width)], out_ref, sem)
    copy.start()
    copy.wait()


def member_slice(weight, width):
    return pl.pallas_call(
        functools.partial(slice_kernel, width),
        in_specs=[ANYWHERE],
        out_specs=IN_VMEM,
        out_shape=jax.ShapeDtypeStruct((width, weight.shape[1]), weight.dtype),
        scratch_shapes=[pltpu.SemaphoreType.DMA],
        cost_estimate=CHEAP,
    )(weight)


def own_kernel(info_ref, up_ref, weight_ref, in_adapter_ref, out_adapter_ref, after_ref, out_ref, token_ref, pair_ref, turned_ref):
    @pl.when(pl.program_id(0) == 0)
    def _():
        pair_ref[...] = split_pair(up_ref[...], out_adapter_ref[...])
        turned_ref[...] = up_ref[...].T
        token_ref[...] = jnp.zeros_like(token_ref)

    total = dot(weight_ref[...], turned_ref[...]).T
    total += dot(pair_ref[...], twice(in_adapter_ref[...]))
    out_ref[...] = total.astype(out_ref.dtype)


def own_columns(info, upstream, weight, adapter_in_t, adapter_out, all_columns, after):
    tokens, depth = upstream.shape
    columns = weight.shape[0]
    block = min(1024, columns)
    steps = columns // block
    rank = adapter_in_t.shape[0]
    return pl.pallas_call(
        own_kernel,
        grid_spec=pltpu.PrefetchScalarGridSpec(
            num_scalar_prefetch=1,
            grid=(steps,),
            in_specs=[
                pl.BlockSpec((tokens, depth), lambda i, s: (0, 0)),
                pl.BlockSpec((block, depth), lambda i, s: (i, 0)),
                pl.BlockSpec((rank, block), lambda i, s: (0, s[0] * steps + i)),
                pl.BlockSpec(adapter_out.shape, lambda i, s: (0, 0)),
                pl.BlockSpec(memory_space=pl.ANY),
            ],
            out_specs=[pl.BlockSpec((tokens, block), lambda i, s: (0, s[0] * steps + i)), TOKEN_BLOCK],
            scratch_shapes=[
                pltpu.VMEM((tokens, 2 * rank), jnp.bfloat16),
                pltpu.VMEM((depth, tokens), jnp.bfloat16),
            ],
        ),
        out_shape=[jax.ShapeDtypeStruct((tokens, all_columns), jnp.bfloat16), TOKEN],
        cost_estimate=CHEAP,
        compiler_params=pltpu.CompilerParams(vmem_limit_bytes=VMEM_BYTES),
    )(info[PLACE].reshape(1), upstream, weight, adapter_in_t, adapter_out, after)


def pair_kernel(chips, *refs):
    out_adapter_ref, after_ref, out_ref = refs[chips:]
    for chip in range(chips):
        out_ref[chip] = split_pair(refs[chip][...], out_adapter_ref[...])


def plane_pairs(plane, adapter_out, after):
    chips = len(plane)
    tokens = plane[0].shape[0]
    return pl.pallas_call(
        functools.partial(pair_kernel, chips),
        in_specs=[IN_VMEM] * (chips + 1) + [ANYWHERE],
        out_specs=IN_VMEM,
        out_shape=jax.ShapeDtypeStruct((chips, tokens, 2 * adapter_out.shape[0]), jnp.bfloat16),
        cost_estimate=DEAR,
        compiler_params=pltpu.CompilerParams(vmem_limit_bytes=VMEM_BYTES),
    )(*plane, adapter_out, after)


def slice_columns(info_ref, shift, half, width, chips, tokens, weight, adapter_ref, pairs):
    at = pl.multiple_of(lax.bitwise_xor(lax.rem(info_ref[MEMBER], 2), half) * width, width)
    here = (info_ref[SHARDS + shift] * chips + info_ref[CHIP]) * 2 * width + at
    total = contract_last(tokens, weight)
    total += dot(pairs, twice(adapter_ref[:, pl.ds(pl.multiple_of(here, width), width)]))
    return at, total.astype(jnp.bfloat16)


def piece_kernel(shifts, chips, groups, *refs):
    info_ref = here(groups)
    others = chips - 1
    token_refs, refs = refs[:others], refs[others:]
    weight_refs, refs = refs[: 2 * len(shifts)], refs[2 * len(shifts) :]
    adapter_ref, pair_ref, _ = refs[:3]
    out_refs, token_ref = refs[3 : 3 + others], refs[3 + others]
    token_ref[...] = jnp.zeros_like(token_ref)
    rows = token_refs[0].shape[0]
    width = weight_refs[0].shape[0]
    stacked = jnp.concatenate([ref[...] for ref in token_refs], axis=0)
    pairs = pair_ref[1:].reshape(others * rows, pair_ref.shape[2])
    for index, shift in enumerate(shifts):
        for half in range(2):
            weight = weight_refs[2 * index + half][...]
            at, total = slice_columns(info_ref, shift, half, width, chips, stacked, weight, adapter_ref, pairs)
            at = pl.multiple_of(at + index * 2 * width, width)
            for k in range(others):
                out_refs[k][:, pl.ds(at, width)] = total[k * rows : (k + 1) * rows]


def plain_columns(info, shift, tokens, weights, adapter_in_t, pairs, chips):
    mine, other = weights
    width = mine.shape[0]
    ordered = [jnp.concatenate([mine, other]), jnp.concatenate([other, mine])]
    both = jnp.where(lax.rem(info[MEMBER], 2) == 0, *ordered)
    at = (info[SHARDS + shift] * chips + info[CHIP]) * 2 * width
    low = twice(lax.dynamic_slice_in_dim(adapter_in_t, at, 2 * width, 1))
    return (contract_last(tokens, both) + dot(pairs, low)).astype(jnp.bfloat16)


def piece_columns(info, shifts, plane, weights, adapter_in_t, pairs, after, cost):
    chips = len(plane)
    tokens = plane[0].shape[0]
    width = weights[0][0].shape[0]
    if width % 128:
        columns = [
            [plain_columns(info, s, plane[k], w, adapter_in_t, pairs[k], chips) for s, w in zip(shifts, weights)]
            for k in range(1, chips)
        ]
        return [jnp.concatenate(c, axis=1) for c in columns], after
    count = len(weights)
    out_shape = jax.ShapeDtypeStruct((tokens, count * 2 * width), jnp.bfloat16)
    outs = pl.pallas_call(
        functools.partial(piece_kernel, shifts, chips, lax.axis_size("fsdp")),
        in_specs=[IN_VMEM] * (chips - 1 + 2 * count + 2) + [ANYWHERE],
        out_specs=[IN_VMEM] * chips,
        out_shape=[out_shape] * (chips - 1) + [TOKEN],
        cost_estimate=cost,
        compiler_params=pltpu.CompilerParams(vmem_limit_bytes=VMEM_BYTES),
    )(*plane[1:], *[w for pair in weights for w in pair], adapter_in_t, pairs, after)
    return outs[:-1], outs[-1]


def place_kernel(shifts, chips, mine, groups, *refs):
    info_ref = here(groups)
    piece_refs, refs = refs[: chips - 1], refs[chips - 1 :]
    if mine:
        up_ref, refs = refs[0], refs[1:]
        weight_refs, refs = refs[: 2 * len(mine)], refs[2 * len(mine) :]
        adapter_ref, pair_ref, refs = refs[0], refs[1], refs[2:]
        mine_ref, refs = refs[-1], refs[:-1]
    out_ref, sems = refs[2:]
    width = piece_refs[0].shape[1] // len(shifts)
    copies = []

    def send(source, at):
        at = pl.multiple_of(at * width, width)
        copies.append(pltpu.make_async_copy(source, out_ref.at[:, pl.ds(at, width)], sems.at[len(copies)]))
        copies[-1].start()

    for index, shift in enumerate(shifts):
        for k in range(1, chips):
            at = info_ref[SHARDS + shift] * chips + lax.bitwise_xor(info_ref[CHIP], k)
            send(piece_refs[k - 1].at[:, pl.ds(index * width, width)], at)
    for index, shift in enumerate(mine):
        for half in range(2):
            at, total = slice_columns(
                info_ref,
                shift,
                half,
                width // 2,
                chips,
                up_ref[...],
                weight_refs[2 * index + half][...],
                adapter_ref,
                pair_ref[0],
            )
            mine_ref[:, pl.ds(pl.multiple_of(at + index * width, width // 2), width // 2)] = total
        send(mine_ref.at[:, pl.ds(index * width, width)], info_ref[SHARDS + shift] * chips + info_ref[CHIP])
    for copy in copies:
        copy.wait()


def place_columns(info, shifts, pieces, buffer, after, cost, mine, upstream, weights, adapter_in_t, pairs):
    chips = len(pieces) + 1
    tokens = pieces[0].shape[0]
    width = pieces[0].shape[1] // len(shifts)
    if width % 128 or width % 256 and mine:
        for index, shift in enumerate(shifts):
            for k, piece in enumerate(pieces, 1):
                part = piece[:, index * width : (index + 1) * width]
                at = (info[SHARDS + shift] * chips + lax.bitwise_xor(info[CHIP], k)) * width
                buffer = lax.dynamic_update_slice_in_dim(buffer, part, at, 1)
        for shift in mine:
            part = plain_columns(info, shift, upstream, weights[shift], adapter_in_t, pairs[0], chips)
            at = (info[SHARDS + shift] * chips + info[CHIP]) * width
            buffer = lax.dynamic_update_slice_in_dim(buffer, part, at, 1)
        return buffer
    extra = []
    if mine:
        extra = [upstream] + [w for shift in mine for w in weights[shift]] + [adapter_in_t, pairs]
    operands = [*pieces, *extra, buffer, after]
    return pl.pallas_call(
        functools.partial(place_kernel, shifts, chips, mine, lax.axis_size("fsdp")),
        in_specs=[IN_VMEM] * (len(operands) - 2) + [ANYWHERE] * 2,
        out_specs=ANYWHERE,
        out_shape=jax.ShapeDtypeStruct(buffer.shape, buffer.dtype),
        scratch_shapes=[pltpu.SemaphoreType.DMA(((chips - 1) * len(shifts) + len(mine),))]
        + ([pltpu.VMEM((tokens, len(mine) * width), jnp.bfloat16)] if mine else []),
        input_output_aliases={len(operands) - 2: 0},
        cost_estimate=cost,
        compiler_params=pltpu.CompilerParams(vmem_limit_bytes=VMEM_BYTES),
    )(*operands)


def flat_kernel(rank, groups, chunk_rows, in_ref, up_ref, in_adapter_ref, out_adapter_ref, out_ref, scaled_ref, narrow_ref, turn_ref, flat_ref, line_ref):
    step = pl.program_id(0)
    tokens, block = in_ref.shape
    model = flat_ref.shape[1] - up_ref.shape[1]

    @pl.when(step == 0)
    def _():
        through = lowrank_scale_factor * contract_last(out_adapter_ref[...], up_ref[...])
        scaled_ref[...] = through.astype(jnp.bfloat16)
        narrow_ref[...] = jnp.zeros_like(narrow_ref)

    at = pl.multiple_of(step * block, block)
    flat_ref[:, pl.ds(at, block)] = dot(scaled_ref[...], in_ref[...])
    narrow_ref[...] += contract_last(in_ref[...], in_adapter_ref[...])

    @pl.when(step == pl.num_programs(0) - 1)
    def _():
        narrow = narrow_ref[...].T.astype(jnp.bfloat16)
        turn_ref[...] = (lowrank_scale_factor * dot(narrow, up_ref[...])).T
        span = up_ref.shape[1] // rank
        lines = [turn_ref[pl.ds(row, span, rank), :].T for row in range(rank)]
        for r in range(rank):
            part = jnp.concatenate([line[r : r + 1] for line in lines], axis=0)
            flat_ref[:, model + r * span : model + (r + 1) * span] = part
        if chunk_rows:
            tiles = flat_ref.shape[1] // 128 // groups
            for place in range(groups):
                for tile in range(tiles):
                    at = (place * tiles + tile) * 128
                    line_ref[pl.ds(place * chunk_rows + tile, rank, groups * chunk_rows), :] = flat_ref[
                        :, at : at + 128
                    ]
            out_ref[...] = line_ref[...].astype(jnp.bfloat16)
        else:
            out_ref[...] = flat_ref[...].astype(jnp.bfloat16)


def pair_gradient(inputs, upstream, adapter_in_t, adapter_out, groups, chunk_rows):
    tokens, model = inputs.shape
    depth = upstream.shape[1]
    rank = adapter_in_t.shape[0]
    steps = 2
    block = model // steps
    out_shape = (rank * groups * chunk_rows, 128) if chunk_rows else (rank, model + depth)
    return pl.pallas_call(
        functools.partial(flat_kernel, rank, groups, chunk_rows),
        grid=(steps,),
        in_specs=[
            pl.BlockSpec((tokens, block), lambda i: (0, i)),
            pl.BlockSpec((tokens, depth), lambda i: (0, 0)),
            pl.BlockSpec((rank, block), lambda i: (0, i)),
            pl.BlockSpec((rank, depth), lambda i: (0, 0)),
        ],
        out_specs=pl.BlockSpec(out_shape, lambda i: (0, 0)),
        out_shape=jax.ShapeDtypeStruct(out_shape, jnp.bfloat16),
        scratch_shapes=[
            pltpu.VMEM((rank, tokens), jnp.bfloat16),
            pltpu.VMEM((tokens, rank), jnp.float32),
            pltpu.VMEM((depth, rank), jnp.float32),
            pltpu.VMEM((rank, model + depth), jnp.float32),
            pltpu.VMEM((max(rank * groups * chunk_rows, 8), 128), jnp.float32),
        ],
        cost_estimate=CHEAP,
    )(inputs, upstream, adapter_in_t, adapter_out)


def project_kernel(stride, chunk, width, chunk_rows, mean_rows, first, seed_ref, part_ref, after_ref, out_ref, token_ref, wide_ref, line_ref, sum_ref):
    devices, rows = wide_ref.shape
    tiles = sum_ref.shape[0] // devices

    @pl.when(pl.program_id(0) == 0)
    def _():
        token_ref[...] = jnp.zeros_like(token_ref)
        if chunk_rows:
            line_ref[...] = part_ref[...].astype(jnp.float32)
            for tile in range(mean_rows):
                line = line_ref[pl.ds(tile, devices, chunk_rows), :]
                wide_ref[:, tile * 128 : (tile + 1) * 128] = line.astype(jnp.bfloat16)
                mean = jnp.sum(line, axis=0, keepdims=True) / devices
                sum_ref[pl.ds(PROJ // 128 + tile, devices, tiles), :] = jnp.broadcast_to(mean, (devices, 128))
        else:
            wide_ref[...] = part_ref[...]

    start = first() * -1640531535 + seed_ref[0] * 668265263
    columns = pl.program_id(0) * width + lax.broadcasted_iota(jnp.int32, (1, width), 1)
    columns = columns * -2048144789
    total = jnp.zeros((devices, width), jnp.float32)
    for at in range(0, rows, chunk):
        count = min(chunk, rows - at)
        lines = lax.broadcasted_iota(jnp.int32, (count, 1), 0) + at
        lines = lines * stride + start
        total += dot(wide_ref[:, at : at + count], hash_signs(lines + columns))
    for tile in range(width // 128):
        at = pl.program_id(0) * (width // 128) + tile
        sum_ref[pl.ds(at, devices, tiles), :] = total[:, tile * 128 : (tile + 1) * 128]

    @pl.when(pl.program_id(0) == pl.num_programs(0) - 1)
    def _():
        out_ref[...] = sum_ref[...].astype(out_ref.dtype)


def project(seed, first, part, stride, after, devices, length, chunk_rows):
    width = PROJ
    mean_rows = length // 128 if chunk_rows else 0
    tiles = PROJ // 128 + -(-mean_rows // 8) * 8
    feats, token = pl.pallas_call(
        functools.partial(project_kernel, stride, 256, width, chunk_rows, mean_rows, first),
        grid_spec=pltpu.PrefetchScalarGridSpec(
            num_scalar_prefetch=1,
            grid=(PROJ // width,),
            in_specs=[pl.BlockSpec(part.shape, lambda i, s: (0, 0)), pl.BlockSpec(memory_space=pl.ANY)],
            out_specs=[pl.BlockSpec((devices * tiles, 128), lambda i, s: (0, 0)), TOKEN_BLOCK],
            scratch_shapes=[
                pltpu.VMEM((devices, length), jnp.bfloat16),
                pltpu.VMEM((max(devices * chunk_rows, 8), 128), jnp.float32),
                pltpu.VMEM((devices * tiles, 128), jnp.float32),
            ],
        ),
        out_shape=[jax.ShapeDtypeStruct((devices * tiles, 128), jnp.bfloat16), TOKEN],
        cost_estimate=DEAR,
        compiler_params=pltpu.CompilerParams(vmem_limit_bytes=VMEM_BYTES),
    )(seed, part, after)
    return feats.reshape(devices, tiles, 128), token


def wrap32(value):
    return (value + 2**31) % 2**32 - 2**31


def per_device(inputs, upstream, value_weight, adapter_in, adapter_out, sign_seed):
    groups, members = lax.axis_size("fsdp"), lax.axis_size("grp")
    place, member = lax.axis_index("fsdp"), lax.axis_index("grp")
    devices = groups * members
    adapter_in_t = adapter_in.T
    rank, model = adapter_in_t.shape
    tokens = inputs.shape[0]
    columns = value_weight.shape[0]
    width = columns // members

    def along(array, shift):
        return lax.ppermute(array, "fsdp", [(i, (i + shift) % groups) for i in range(groups)])

    def across(array, mask):
        return lax.ppermute(array, "grp", [(i, i ^ mask) for i in range(members)])

    slice_own = member_slice(value_weight, width)
    shifts = sorted(range(1, groups), key=lambda s: (min(s, groups - s), s))
    weights = {}
    for s in shifts:
        if s in (1, groups - 1):
            weights[s] = along(slice_own, s)
        elif s <= groups // 2:
            weights[s] = along(weights[s - 1], 1)
        else:
            weights[s] = along(weights[s + 1], -1)
    chips = members // 2
    chip = member // 2
    plane = [across(upstream, 2 * k) if k else upstream for k in range(chips)]

    share = (model + upstream.shape[1]) // groups
    length = rank * share // members
    assert members % rank == 0
    split = members // rank
    info = here(groups)

    def first_parameter():
        member, place = here(groups)[:2]
        row = lax.div(member, split)
        column = place * share + lax.rem(member, split) * length
        return column * rank + row

    chunk_rows = 0 if length % 128 or split > 1 else -(-length // 1024) * 8
    flat = pair_gradient(inputs, upstream, adapter_in_t, adapter_out, groups, chunk_rows)
    both = ("grp", "fsdp")
    if chunk_rows:
        chunks = flat.reshape(devices, chunk_rows, 128)
    else:
        chunks = flat.reshape(rank, groups, split, length).swapaxes(1, 2).reshape(devices, length)
    received = lax.all_to_all(chunks, both, split_axis=0, concat_axis=0, tiled=True)
    if chunk_rows:
        received = received.reshape(devices * chunk_rows, 128)

    result, token = own_columns(info, upstream, value_weight, adapter_in_t, adapter_out, groups * columns, flat)

    near = [s for s in shifts if s in (1, groups - 1)]
    batches = [near] + [[s] for s in shifts if s not in near]
    pairs = plane_pairs(plane, adapter_out, token)
    after, sent, feats = pairs, [], None
    slices = {s: (weights[s], across(weights[s], 1)) for s in shifts}
    for batch in batches:
        pieces, token = piece_columns(
            info,
            batch,
            plane,
            [slices[s] for s in batch],
            adapter_in_t,
            pairs,
            after,
            CHEAP,
        )
        sent.append((batch, [across(p, 2 * k) for k, p in enumerate(pieces, 1)]))
        if feats is None:
            feats, token = project(
                sign_seed,
                first_parameter,
                received,
                wrap32(-1640531535 * rank),
                token,
                devices,
                length,
                chunk_rows,
            )
            after = token
    parts = lax.all_to_all(feats, both, split_axis=0, concat_axis=0, tiled=True)
    raw = jnp.sum(parts[:, : PROJ // 128].astype(jnp.float32), axis=0)
    features = (raw * lax.rsqrt(jnp.mean(raw * raw) + 1e-06)).reshape(1, PROJ)
    mean_rows = length // 128
    if chunk_rows:
        totals = parts.reshape(members, groups, -1, 128)[:, :, PROJ // 128 : PROJ // 128 + mean_rows]
        totals = lax.dynamic_index_in_dim(totals, place, 1, keepdims=False).astype(jnp.float32)
    else:
        local_total = jnp.sum(received.astype(jnp.float32), axis=0) / devices
        totals = lax.all_to_all(
            jnp.broadcast_to(local_total, (members, length)), "grp", split_axis=0, concat_axis=0, tiled=True
        )
    mean_grad = totals.reshape(rank, share).T.reshape(-1)

    for index, (batch, pieces) in enumerate(sent):
        first, last = index == 0, index == len(sent) - 1
        result = place_columns(
            info,
            batch,
            pieces,
            result,
            features if last else token,
            CHEAP if last else DEAR,
            shifts if first else [],
            upstream,
            slices,
            adapter_in_t,
            pairs,
        )
    return (result, features, mean_grad)


def solution(mesh):
    return jax.shard_map(
        per_device,
        mesh=mesh,
        in_specs=(
            P(("grp", "fsdp"), None),
            P(("grp", "fsdp"), None),
            P("fsdp", None),
            P(),
            P(),
            P(),
        ),
        out_specs=(P(("grp", "fsdp"), None), P(("grp", "fsdp"), None), P("fsdp")),
        check_vma=False,
    )
```

```python
import functools

import jax
import jax.numpy as jnp
from jax import lax
from jax.experimental import pallas as pl
from jax.experimental.pallas import tpu as pltpu
from jax.sharding import PartitionSpec as P

PROJ = 4096

lowrank_scale_factor = 2.0

CHEAP = pl.CostEstimate(flops=0, bytes_accessed=0, transcendentals=0)
VMEM_BYTES = 24 * 2**20
MEMBER, PLACE, CHIP, SHARDS = range(4)
DEAR = pl.CostEstimate(flops=10**11, bytes_accessed=0, transcendentals=0)


def contract_last(left, right):
    return lax.dot_general(
        left, right, (((1,), (1,)), ((), ())), preferred_element_type=jnp.float32
    )


def dot(left, right):
    return jnp.dot(left, right, preferred_element_type=jnp.float32)


def hash_signs(mixed):
    mixed = mixed ^ lax.shift_right_logical(mixed, 15)
    mixed = mixed * 181057748
    mixed = mixed ^ lax.shift_left(mixed, 13)
    return jnp.where(mixed < 0, jnp.bfloat16(-1.0), jnp.bfloat16(1.0))


def split_pair(tokens, adapter_out):
    through = lowrank_scale_factor * contract_last(tokens, adapter_out)
    high = through.astype(jnp.bfloat16)
    low = (through - high.astype(jnp.float32)).astype(jnp.bfloat16)
    return jnp.concatenate([high, low], axis=1)


ANYWHERE = pl.BlockSpec(memory_space=pl.ANY)
IN_VMEM = pl.BlockSpec(memory_space=pltpu.VMEM)
IN_SMEM = pl.BlockSpec(memory_space=pltpu.SMEM)
TOKEN = jax.ShapeDtypeStruct((8, 128), jnp.float32)
TOKEN_BLOCK = pl.BlockSpec((8, 128), lambda *_: (0, 0))


def twice(part):
    return jnp.concatenate([part, part], axis=0)


def here(groups):
    member, place = lax.axis_index("grp"), lax.axis_index("fsdp")
    return [member, place, lax.div(member, 2)] + [lax.rem(place + groups - s, groups) for s in range(groups)]


def slice_kernel(width, weight_ref, out_ref, held_ref, sems):
    start = lax.axis_index("grp") * width
    rows = held_ref.shape[1]
    parts = held_ref.shape[0]
    taken, sent = [], []
    for part in range(parts):
        at = pl.multiple_of(start + part * rows, rows)
        taken.append(pltpu.make_async_copy(weight_ref.at[pl.ds(at, rows)], held_ref.at[part], sems.at[0, part]))
        taken[-1].start()
    for part in range(parts):
        taken[part].wait()
        sent.append(
            pltpu.make_async_copy(held_ref.at[part], out_ref.at[pl.ds(part * rows, rows)], sems.at[1, part])
        )
        sent[-1].start()
    for copy in sent:
        copy.wait()


def member_slice(weight, width):
    parts = 4 if width % 128 == 0 else 1
    return pl.pallas_call(
        functools.partial(slice_kernel, width),
        in_specs=[ANYWHERE],
        out_specs=ANYWHERE,
        out_shape=jax.ShapeDtypeStruct((width, weight.shape[1]), weight.dtype),
        scratch_shapes=[
            pltpu.VMEM((parts, width // parts, weight.shape[1]), weight.dtype),
            pltpu.SemaphoreType.DMA((2, parts)),
        ],
        cost_estimate=CHEAP,
    )(weight)


def own_kernel(info_ref, up_ref, weight_ref, in_adapter_ref, out_adapter_ref, after_ref, out_ref, token_ref, pair_ref, turned_ref):
    @pl.when(pl.program_id(0) == 0)
    def _():
        pair_ref[...] = split_pair(up_ref[...], out_adapter_ref[...])
        turned_ref[...] = up_ref[...].T
        token_ref[...] = jnp.zeros_like(token_ref)

    total = dot(weight_ref[...], turned_ref[...]).T
    total += dot(pair_ref[...], twice(in_adapter_ref[...]))
    out_ref[...] = total.astype(out_ref.dtype)


def own_columns(info, upstream, weight, adapter_in_t, adapter_out, all_columns, after):
    tokens, depth = upstream.shape
    columns = weight.shape[0]
    block = min(1024, columns)
    steps = columns // block
    rank = adapter_in_t.shape[0]
    return pl.pallas_call(
        own_kernel,
        grid_spec=pltpu.PrefetchScalarGridSpec(
            num_scalar_prefetch=1,
            grid=(steps,),
            in_specs=[
                pl.BlockSpec((tokens, depth), lambda i, s: (0, 0)),
                pl.BlockSpec((block, depth), lambda i, s: (i, 0)),
                pl.BlockSpec((rank, block), lambda i, s: (0, s[0] * steps + i)),
                pl.BlockSpec(adapter_out.shape, lambda i, s: (0, 0)),
                pl.BlockSpec(memory_space=pl.ANY),
            ],
            out_specs=[pl.BlockSpec((tokens, block), lambda i, s: (0, s[0] * steps + i)), TOKEN_BLOCK],
            scratch_shapes=[
                pltpu.VMEM((tokens, 2 * rank), jnp.bfloat16),
                pltpu.VMEM((depth, tokens), jnp.bfloat16),
            ],
        ),
        out_shape=[jax.ShapeDtypeStruct((tokens, all_columns), jnp.bfloat16), TOKEN],
        cost_estimate=CHEAP,
        compiler_params=pltpu.CompilerParams(vmem_limit_bytes=VMEM_BYTES),
    )(info[PLACE].reshape(1), upstream, weight, adapter_in_t, adapter_out, after)


def pair_kernel(chips, *refs):
    out_adapter_ref, after_ref, out_ref = refs[chips:]
    for chip in range(chips):
        out_ref[chip] = split_pair(refs[chip][...], out_adapter_ref[...])


def plane_pairs(plane, adapter_out, after):
    chips = len(plane)
    tokens = plane[0].shape[0]
    return pl.pallas_call(
        functools.partial(pair_kernel, chips),
        in_specs=[IN_VMEM] * (chips + 1) + [ANYWHERE],
        out_specs=IN_VMEM,
        out_shape=jax.ShapeDtypeStruct((chips, tokens, 2 * adapter_out.shape[0]), jnp.bfloat16),
        cost_estimate=DEAR,
        compiler_params=pltpu.CompilerParams(vmem_limit_bytes=VMEM_BYTES),
    )(*plane, adapter_out, after)


def slice_columns(info_ref, shift, half, width, chips, tokens, weight, adapter_ref, pairs):
    at = pl.multiple_of(lax.bitwise_xor(lax.rem(info_ref[MEMBER], 2), half) * width, width)
    here = (info_ref[SHARDS + shift] * chips + info_ref[CHIP]) * 2 * width + at
    total = contract_last(tokens, weight)
    total += dot(pairs, twice(adapter_ref[:, pl.ds(pl.multiple_of(here, width), width)]))
    return at, total.astype(jnp.bfloat16)


def piece_kernel(shifts, chips, groups, *refs):
    info_ref = here(groups)
    others = chips - 1
    token_refs, refs = refs[:others], refs[others:]
    weight_refs, refs = refs[: 2 * len(shifts)], refs[2 * len(shifts) :]
    adapter_ref, pair_ref, _ = refs[:3]
    out_refs, token_ref = refs[3 : 3 + others], refs[3 + others]
    token_ref[...] = jnp.zeros_like(token_ref)
    rows = token_refs[0].shape[0]
    width = weight_refs[0].shape[0]
    stacked = jnp.concatenate([ref[...] for ref in token_refs], axis=0)
    pairs = pair_ref[1:].reshape(others * rows, pair_ref.shape[2])
    for index, shift in enumerate(shifts):
        for half in range(2):
            weight = weight_refs[2 * index + half][...]
            at, total = slice_columns(info_ref, shift, half, width, chips, stacked, weight, adapter_ref, pairs)
            at = pl.multiple_of(at + index * 2 * width, width)
            for k in range(others):
                out_refs[k][:, pl.ds(at, width)] = total[k * rows : (k + 1) * rows]


def plain_columns(info, shift, tokens, weights, adapter_in_t, pairs, chips):
    mine, other = weights
    width = mine.shape[0]
    ordered = [jnp.concatenate([mine, other]), jnp.concatenate([other, mine])]
    both = jnp.where(lax.rem(info[MEMBER], 2) == 0, *ordered)
    at = (info[SHARDS + shift] * chips + info[CHIP]) * 2 * width
    low = twice(lax.dynamic_slice_in_dim(adapter_in_t, at, 2 * width, 1))
    return (contract_last(tokens, both) + dot(pairs, low)).astype(jnp.bfloat16)


def piece_columns(info, shifts, plane, weights, adapter_in_t, pairs, after, cost):
    chips = len(plane)
    tokens = plane[0].shape[0]
    width = weights[0][0].shape[0]
    if width % 128:
        columns = [
            [plain_columns(info, s, plane[k], w, adapter_in_t, pairs[k], chips) for s, w in zip(shifts, weights)]
            for k in range(1, chips)
        ]
        return [jnp.concatenate(c, axis=1) for c in columns], after
    count = len(weights)
    out_shape = jax.ShapeDtypeStruct((tokens, count * 2 * width), jnp.bfloat16)
    outs = pl.pallas_call(
        functools.partial(piece_kernel, shifts, chips, lax.axis_size("fsdp")),
        in_specs=[IN_VMEM] * (chips - 1 + 2 * count + 2) + [ANYWHERE],
        out_specs=[IN_VMEM] * chips,
        out_shape=[out_shape] * (chips - 1) + [TOKEN],
        cost_estimate=cost,
        compiler_params=pltpu.CompilerParams(vmem_limit_bytes=VMEM_BYTES),
    )(*plane[1:], *[w for pair in weights for w in pair], adapter_in_t, pairs, after)
    return outs[:-1], outs[-1]


def place_kernel(shifts, chips, mine, groups, *refs):
    info_ref = here(groups)
    piece_refs, refs = refs[: chips - 1], refs[chips - 1 :]
    if mine:
        up_ref, refs = refs[0], refs[1:]
        weight_refs, refs = refs[: 2 * len(mine)], refs[2 * len(mine) :]
        adapter_ref, pair_ref, refs = refs[0], refs[1], refs[2:]
        mine_ref, refs = refs[-1], refs[:-1]
    out_ref, sems = refs[2:]
    width = piece_refs[0].shape[1] // len(shifts)
    copies = []

    def send(source, at):
        at = pl.multiple_of(at * width, width)
        copies.append(pltpu.make_async_copy(source, out_ref.at[:, pl.ds(at, width)], sems.at[len(copies)]))
        copies[-1].start()

    for index, shift in enumerate(shifts):
        for k in range(1, chips):
            at = info_ref[SHARDS + shift] * chips + lax.bitwise_xor(info_ref[CHIP], k)
            send(piece_refs[k - 1].at[:, pl.ds(index * width, width)], at)
    for index, shift in enumerate(mine):
        for half in range(2):
            at, total = slice_columns(
                info_ref,
                shift,
                half,
                width // 2,
                chips,
                up_ref[...],
                weight_refs[2 * index + half][...],
                adapter_ref,
                pair_ref[0],
            )
            mine_ref[:, pl.ds(pl.multiple_of(at + index * width, width // 2), width // 2)] = total
        send(mine_ref.at[:, pl.ds(index * width, width)], info_ref[SHARDS + shift] * chips + info_ref[CHIP])
    for copy in copies:
        copy.wait()


def place_columns(info, shifts, pieces, buffer, after, cost, mine, upstream, weights, adapter_in_t, pairs):
    chips = len(pieces) + 1
    tokens = pieces[0].shape[0]
    width = pieces[0].shape[1] // len(shifts)
    if width % 128 or width % 256 and mine:
        for index, shift in enumerate(shifts):
            for k, piece in enumerate(pieces, 1):
                part = piece[:, index * width : (index + 1) * width]
                at = (info[SHARDS + shift] * chips + lax.bitwise_xor(info[CHIP], k)) * width
                buffer = lax.dynamic_update_slice_in_dim(buffer, part, at, 1)
        for shift in mine:
            part = plain_columns(info, shift, upstream, weights[shift], adapter_in_t, pairs[0], chips)
            at = (info[SHARDS + shift] * chips + info[CHIP]) * width
            buffer = lax.dynamic_update_slice_in_dim(buffer, part, at, 1)
        return buffer
    extra = []
    if mine:
        extra = [upstream] + [w for shift in mine for w in weights[shift]] + [adapter_in_t, pairs]
    operands = [*pieces, *extra, buffer, after]
    return pl.pallas_call(
        functools.partial(place_kernel, shifts, chips, mine, lax.axis_size("fsdp")),
        in_specs=[IN_VMEM] * (len(operands) - 2) + [ANYWHERE] * 2,
        out_specs=ANYWHERE,
        out_shape=jax.ShapeDtypeStruct(buffer.shape, buffer.dtype),
        scratch_shapes=[pltpu.SemaphoreType.DMA(((chips - 1) * len(shifts) + len(mine),))]
        + ([pltpu.VMEM((tokens, len(mine) * width), jnp.bfloat16)] if mine else []),
        input_output_aliases={len(operands) - 2: 0},
        cost_estimate=cost,
        compiler_params=pltpu.CompilerParams(vmem_limit_bytes=VMEM_BYTES),
    )(*operands)


def flat_kernel(rank, groups, chunk_rows, in_ref, up_ref, in_adapter_ref, out_adapter_ref, out_ref, scaled_ref, narrow_ref, turn_ref, flat_ref, line_ref):
    step = pl.program_id(0)
    tokens, block = in_ref.shape
    model = flat_ref.shape[1] - up_ref.shape[1]

    @pl.when(step == 0)
    def _():
        through = lowrank_scale_factor * contract_last(out_adapter_ref[...], up_ref[...])
        scaled_ref[...] = through.astype(jnp.bfloat16)
        narrow_ref[...] = jnp.zeros_like(narrow_ref)

    at = pl.multiple_of(step * block, block)
    flat_ref[:, pl.ds(at, block)] = dot(scaled_ref[...], in_ref[...])
    narrow_ref[...] += contract_last(in_ref[...], in_adapter_ref[...])

    @pl.when(step == pl.num_programs(0) - 1)
    def _():
        narrow = narrow_ref[...].T.astype(jnp.bfloat16)
        turn_ref[...] = (lowrank_scale_factor * dot(narrow, up_ref[...])).T
        span = up_ref.shape[1] // rank
        lines = [turn_ref[pl.ds(row, span, rank), :].T for row in range(rank)]
        for r in range(rank):
            part = jnp.concatenate([line[r : r + 1] for line in lines], axis=0)
            flat_ref[:, model + r * span : model + (r + 1) * span] = part
        if chunk_rows:
            tiles = flat_ref.shape[1] // 128 // groups
            for place in range(groups):
                for tile in range(tiles):
                    at = (place * tiles + tile) * 128
                    line_ref[pl.ds(place * chunk_rows + tile, rank, groups * chunk_rows), :] = flat_ref[
                        :, at : at + 128
                    ]
            out_ref[...] = line_ref[...].astype(jnp.bfloat16)
        else:
            out_ref[...] = flat_ref[...].astype(jnp.bfloat16)


def pair_gradient(inputs, upstream, adapter_in_t, adapter_out, groups, chunk_rows):
    tokens, model = inputs.shape
    depth = upstream.shape[1]
    rank = adapter_in_t.shape[0]
    steps = 2
    block = model // steps
    out_shape = (rank * groups * chunk_rows, 128) if chunk_rows else (rank, model + depth)
    return pl.pallas_call(
        functools.partial(flat_kernel, rank, groups, chunk_rows),
        grid=(steps,),
        in_specs=[
            pl.BlockSpec((tokens, block), lambda i: (0, i)),
            pl.BlockSpec((tokens, depth), lambda i: (0, 0)),
            pl.BlockSpec((rank, block), lambda i: (0, i)),
            pl.BlockSpec((rank, depth), lambda i: (0, 0)),
        ],
        out_specs=pl.BlockSpec(out_shape, lambda i: (0, 0)),
        out_shape=jax.ShapeDtypeStruct(out_shape, jnp.bfloat16),
        scratch_shapes=[
            pltpu.VMEM((rank, tokens), jnp.bfloat16),
            pltpu.VMEM((tokens, rank), jnp.float32),
            pltpu.VMEM((depth, rank), jnp.float32),
            pltpu.VMEM((rank, model + depth), jnp.float32),
            pltpu.VMEM((max(rank * groups * chunk_rows, 8), 128), jnp.float32),
        ],
        cost_estimate=CHEAP,
    )(inputs, upstream, adapter_in_t, adapter_out)


def project_kernel(stride, chunk, width, chunk_rows, mean_rows, first, seed_ref, part_ref, after_ref, out_ref, token_ref, wide_ref, line_ref, sum_ref):
    devices, rows = wide_ref.shape
    tiles = sum_ref.shape[0] // devices

    @pl.when(pl.program_id(0) == 0)
    def _():
        token_ref[...] = jnp.zeros_like(token_ref)
        if chunk_rows:
            line_ref[...] = part_ref[...].astype(jnp.float32)
            for tile in range(mean_rows):
                line = line_ref[pl.ds(tile, devices, chunk_rows), :]
                wide_ref[:, tile * 128 : (tile + 1) * 128] = line.astype(jnp.bfloat16)
                mean = jnp.sum(line, axis=0, keepdims=True) / devices
                sum_ref[pl.ds(PROJ // 128 + tile, devices, tiles), :] = jnp.broadcast_to(mean, (devices, 128))
        else:
            wide_ref[...] = part_ref[...]

    start = first() * -1640531535 + seed_ref[0] * 668265263
    columns = pl.program_id(0) * width + lax.broadcasted_iota(jnp.int32, (1, width), 1)
    columns = columns * -2048144789
    total = jnp.zeros((devices, width), jnp.float32)
    for at in range(0, rows, chunk):
        count = min(chunk, rows - at)
        lines = lax.broadcasted_iota(jnp.int32, (count, 1), 0) + at
        lines = lines * stride + start
        total += dot(wide_ref[:, at : at + count], hash_signs(lines + columns))
    for tile in range(width // 128):
        at = pl.program_id(0) * (width // 128) + tile
        sum_ref[pl.ds(at, devices, tiles), :] = total[:, tile * 128 : (tile + 1) * 128]

    @pl.when(pl.program_id(0) == pl.num_programs(0) - 1)
    def _():
        out_ref[...] = sum_ref[...].astype(out_ref.dtype)


def project(seed, first, part, stride, after, devices, length, chunk_rows):
    width = PROJ
    mean_rows = length // 128 if chunk_rows else 0
    tiles = PROJ // 128 + -(-mean_rows // 8) * 8
    feats, token = pl.pallas_call(
        functools.partial(project_kernel, stride, 256, width, chunk_rows, mean_rows, first),
        grid_spec=pltpu.PrefetchScalarGridSpec(
            num_scalar_prefetch=1,
            grid=(PROJ // width,),
            in_specs=[pl.BlockSpec(part.shape, lambda i, s: (0, 0)), pl.BlockSpec(memory_space=pl.ANY)],
            out_specs=[pl.BlockSpec((devices * tiles, 128), lambda i, s: (0, 0)), TOKEN_BLOCK],
            scratch_shapes=[
                pltpu.VMEM((devices, length), jnp.bfloat16),
                pltpu.VMEM((max(devices * chunk_rows, 8), 128), jnp.float32),
                pltpu.VMEM((devices * tiles, 128), jnp.float32),
            ],
        ),
        out_shape=[jax.ShapeDtypeStruct((devices * tiles, 128), jnp.bfloat16), TOKEN],
        cost_estimate=DEAR,
    )(seed, part, after)
    return feats.reshape(devices, tiles, 128), token


def wrap32(value):
    return (value + 2**31) % 2**32 - 2**31


def per_device(inputs, upstream, value_weight, adapter_in, adapter_out, sign_seed):
    groups, members = lax.axis_size("fsdp"), lax.axis_size("grp")
    place, member = lax.axis_index("fsdp"), lax.axis_index("grp")
    devices = groups * members
    adapter_in_t = adapter_in.T
    rank, model = adapter_in_t.shape
    tokens = inputs.shape[0]
    columns = value_weight.shape[0]
    width = columns // members

    def along(array, shift):
        return lax.ppermute(array, "fsdp", [(i, (i + shift) % groups) for i in range(groups)])

    def across(array, mask):
        return lax.ppermute(array, "grp", [(i, i ^ mask) for i in range(members)])

    slice_own = member_slice(value_weight, width)
    shifts = sorted(range(1, groups), key=lambda s: (min(s, groups - s), s))
    weights = {}
    for s in shifts:
        if s in (1, groups - 1):
            weights[s] = along(slice_own, s)
        elif s <= groups // 2:
            weights[s] = along(weights[s - 1], 1)
        else:
            weights[s] = along(weights[s + 1], -1)
    chips = members // 2
    chip = member // 2
    plane = [across(upstream, 2 * k) if k else upstream for k in range(chips)]

    share = (model + upstream.shape[1]) // groups
    length = rank * share // members
    assert members % rank == 0
    split = members // rank
    info = here(groups)

    def first_parameter():
        member, place = here(groups)[:2]
        row = lax.div(member, split)
        column = place * share + lax.rem(member, split) * length
        return column * rank + row

    chunk_rows = 0 if length % 128 or split > 1 else -(-length // 1024) * 8
    flat = pair_gradient(inputs, upstream, adapter_in_t, adapter_out, groups, chunk_rows)
    both = ("grp", "fsdp")
    if chunk_rows:
        chunks = flat.reshape(devices, chunk_rows, 128)
    else:
        chunks = flat.reshape(rank, groups, split, length).swapaxes(1, 2).reshape(devices, length)
    received = lax.all_to_all(chunks, both, split_axis=0, concat_axis=0, tiled=True)
    if chunk_rows:
        received = received.reshape(devices * chunk_rows, 128)

    result, token = own_columns(info, upstream, value_weight, adapter_in_t, adapter_out, groups * columns, flat)

    near = [s for s in shifts if s in (1, groups - 1)]
    batches = [near] + [[s] for s in shifts if s not in near]
    pairs = plane_pairs(plane, adapter_out, token)
    after, sent, feats = pairs, [], None
    slices = {s: (weights[s], across(weights[s], 1)) for s in shifts}
    for batch in batches:
        pieces, token = piece_columns(
            info,
            batch,
            plane,
            [slices[s] for s in batch],
            adapter_in_t,
            pairs,
            after,
            CHEAP,
        )
        sent.append((batch, [across(p, 2 * k) for k, p in enumerate(pieces, 1)]))
        if feats is None:
            feats, token = project(
                sign_seed,
                first_parameter,
                received,
                wrap32(-1640531535 * rank),
                token,
                devices,
                length,
                chunk_rows,
            )
            after = token
    parts = lax.all_to_all(feats, both, split_axis=0, concat_axis=0, tiled=True)
    raw = jnp.sum(parts[:, : PROJ // 128].astype(jnp.float32), axis=0)
    features = (raw * lax.rsqrt(jnp.mean(raw * raw) + 1e-06)).reshape(1, PROJ)
    mean_rows = length // 128
    if chunk_rows:
        totals = parts.reshape(members, groups, -1, 128)[:, :, PROJ // 128 : PROJ // 128 + mean_rows]
        totals = lax.dynamic_index_in_dim(totals, place, 1, keepdims=False).astype(jnp.float32)
    else:
        local_total = jnp.sum(received.astype(jnp.float32), axis=0) / devices
        totals = lax.all_to_all(
            jnp.broadcast_to(local_total, (members, length)), "grp", split_axis=0, concat_axis=0, tiled=True
        )
    mean_grad = totals.reshape(rank, share).T.reshape(-1)

    for index, (batch, pieces) in enumerate(sent):
        first, last = index == 0, index == len(sent) - 1
        result = place_columns(
            info,
            batch,
            pieces,
            result,
            features if last else token,
            CHEAP if last else DEAR,
            shifts if first else [],
            upstream,
            slices,
            adapter_in_t,
            pairs,
        )
    return (result, features, mean_grad)


def solution(mesh):
    return jax.shard_map(
        per_device,
        mesh=mesh,
        in_specs=(
            P(("grp", "fsdp"), None),
            P(("grp", "fsdp"), None),
            P("fsdp", None),
            P(),
            P(),
            P(),
        ),
        out_specs=(P(("grp", "fsdp"), None), P(("grp", "fsdp"), None), P("fsdp")),
        check_vma=False,
    )
```
